256 devices in a mesh: gx: 16 (over z_hi, y), gy: 8 (over x, z_lo), gz: 2 (over core).
Axes of the slice: x: 4, y: 4, z: 8 (z_hi: 4, z_lo: 2; z = z_hi * 2 + z_lo), core: 2. Of those that a mesh axis runs over, the one named last changes fastest.
Arguments:
- tensor_blocks: bfloat16 [16, 8, 2, 2, 128, 128, 128], P('gx', 'gy', 'gz'), may hold values from -3072 to 3072
- block_coords: int32 [16, 8, 2, 2, 3], P('gx', 'gy', 'gz'), may hold values from 0 to 1, as said below
- live_counts: int32 [16, 8, 2], P('gx', 'gy', 'gz'), may hold values from 1 to 2, as said below
- factor_a: bfloat16 [16, 256, 256], P('gx', ('gy', 'gz')), may hold values from 0.049804688 to 1
- factor_b: bfloat16 [8, 256, 256], P('gy', ('gx', 'gz')), may hold values from 0.049804688 to 1
- factor_c: bfloat16 [2, 256, 256], P('gz', ('gx', 'gy')), may hold values from 0.049804688 to 1
Outputs:
- updated_a: bfloat16 [16, 256, 256], P('gx', ('gy', 'gz'))
- updated_b: bfloat16 [8, 256, 256], P('gy', ('gx', 'gz'))
- updated_c: bfloat16 [2, 256, 256], P('gz', ('gx', 'gy'))
The draws below stay inside these ranges and needn't reach their ends.
Inputs may be any that keep to these rules, and one draw needn't show every extreme that they name: `block_coords`: within one cell the 2 slots hold distinct positions. `live_counts`: some cell has exactly 2 live slots and another exactly one.
All inputs are finite; a program needn't handle non-finite values. Where the reference program divides by a largest or mean magnitude, that divisor is 1e-20 or more.
Results may differ from the reference program's by a relative error of at most 0.0055.
Values may be sent and summed in bfloat16 or wider, within the bound.
A program may use at most 256 MiB of HBM per device.

```python
import jax
import jax.numpy as jnp
from jax import lax

R = 256
BS = 128
CB = 2
NB_DEV = 2
NS_STEPS = 8
ADMM_ITERS = 4
SLAB = 256
N_GX = 16
N_GY = 8
N_GZ = 2


def draw_block_coords(key, part):
    devices = N_GX * N_GY * N_GZ
    key_list = jax.random.split(key, devices)

    def pick_slots(subkey):
        return jax.random.permutation(subkey, CB * CB * CB)[:NB_DEV]
    chosen = jax.vmap(pick_slots)(key_list)
    triples = jnp.stack([chosen // (CB * CB), chosen // CB % CB, chosen % CB], axis=-1)
    return triples.reshape(N_GX, N_GY, N_GZ, NB_DEV, 3).astype(jnp.int32)


def draw_live_counts(key, part):
    devices = N_GX * N_GY * N_GZ
    counts = jax.random.randint(jax.random.fold_in(key, 11), (devices,), 1, NB_DEV + 1)
    shuffle = jax.random.permutation(jax.random.fold_in(key, 12), devices)
    counts = counts.at[shuffle[0]].set(NB_DEV).at[shuffle[1]].set(1)
    return counts.reshape(N_GX, N_GY, N_GZ).astype(jnp.int32)


def block_scale(key, shape, cuts, low, largest):
    factor_of = 1.0
    for axis_at, blocks in cuts:
        draws = jax.random.uniform(jax.random.fold_in(jax.random.fold_in(key, 6), axis_at), (blocks,), jnp.float32, low / len(cuts), largest / len(cuts))
        factor_of = factor_of * jnp.repeat(jnp.exp(draws), shape[axis_at] // blocks).reshape((-1,) + (1,) * (len(shape) - 1 - axis_at))
    return factor_of


def noise(rng, extent, spread, most, cuts=(), kind=jnp.bfloat16):
    loudness = block_scale(rng, extent, cuts, -0.22, 0.18) if cuts else 1.0
    values = jax.random.normal(rng, extent, jnp.float32) * spread * loudness
    return jnp.minimum(jnp.maximum(values, -most), most).astype(kind)


def setup_inputs(seed: int = 0) -> dict:
    splits = jax.random.split(jax.random.key(seed), 7)
    return {
        "tensor_blocks": noise(splits[0], (N_GX, N_GY, N_GZ, NB_DEV, BS, BS, BS), (CB * CB * BS * N_GY * N_GZ // 16), 3072.0, ((0, 16), (1, 8), (2, 2))),
        "block_coords": draw_block_coords(jax.random.fold_in(splits[6], 71), 0),
        "live_counts": draw_live_counts(jax.random.fold_in(splits[6], 71), 0),
        "factor_a": jnp.clip(0.049804688 + 0.9501953 * jax.random.uniform(splits[3], (N_GX, SLAB, R), jnp.float32) ** block_scale(splits[3], (N_GX, SLAB, R), ((0, 16), (1, 16)), -0.2, 0.2), 0.049804688, 1.0).astype(jnp.bfloat16),
        "factor_b": jnp.clip(0.049804688 + 0.9501953 * jax.random.uniform(splits[4], (N_GY, SLAB, R), jnp.float32) ** block_scale(splits[4], (N_GY, SLAB, R), ((0, 8), (1, 32)), -0.2, 0.2), 0.049804688, 1.0).astype(jnp.bfloat16),
        "factor_c": jnp.clip(0.049804688 + 0.9501953 * jax.random.uniform(splits[5], (N_GZ, SLAB, R), jnp.float32) ** block_scale(splits[5], (N_GZ, SLAB, R), ((0, 2), (1, 128)), -0.2, 0.2), 0.049804688, 1.0).astype(jnp.bfloat16),
    }


HIGHEST = lax.Precision.HIGHEST


def gram_rows(factor):
    return lax.dot_general(factor, factor, (((0,), (0,)), ((), ())), preferred_element_type=jnp.float32)


def newton_inverse(gram_left, gram_right):
    weighted = gram_left * gram_right
    width = weighted.shape[0]
    identity = jnp.eye(width, dtype=weighted.dtype)
    penalty = jnp.trace(weighted) / width
    system = weighted + penalty * identity
    bound = jnp.max(jnp.sum(jnp.abs(system), axis=1))
    inverse = identity / bound
    for step in range(NS_STEPS):
        inverse = jnp.dot(inverse, 2.0 * identity - jnp.dot(system, inverse, precision=HIGHEST), precision=HIGHEST)
    return penalty, inverse


def split_updates(totals, start, penalty, inverse):
    primal = start.astype(jnp.float32)
    dual = jnp.zeros_like(primal)
    for step in range(ADMM_ITERS):
        target = jnp.dot(totals + penalty * (primal + dual), inverse, precision=HIGHEST)
        primal = jnp.maximum(target - dual, 0.0)
        dual = dual + primal - target
    return primal.astype(jnp.bfloat16)


def walk(tensor_blocks, block_coords, live_counts, running, contribution):
    slot_count = tensor_blocks.shape[3]
    side = tensor_blocks.shape[4]
    flat = tensor_blocks.reshape(-1, side, side, side)
    triples = block_coords.reshape(-1, 3)
    counts = live_counts.reshape(-1)
    slab = CB * side

    def visit(position, totals):
        block = lax.dynamic_index_in_dim(flat, position, 0, keepdims=False)
        triple = lax.dynamic_index_in_dim(triples, position, 0, keepdims=False)
        device = position // slot_count
        slot = position % slot_count
        grid_x = device // (N_GY * N_GZ)
        grid_y = (device // N_GZ) % N_GY
        grid_z = device % N_GZ
        starts = ((grid_x * slab + triple[0] * side).astype(jnp.int32),
                  (grid_y * slab + triple[1] * side).astype(jnp.int32),
                  (grid_z * slab + triple[2] * side).astype(jnp.int32))
        target, terms = contribution(block, starts)
        weight = (slot < counts[device]).astype(jnp.float32)
        current = lax.dynamic_slice_in_dim(totals, target, side, 0)
        return lax.dynamic_update_slice_in_dim(totals, current + weight * terms, target, 0)

    return lax.fori_loop(0, flat.shape[0], visit, running)


def reference(tensor_blocks, block_coords, live_counts, factor_a, factor_b, factor_c):
    width = factor_a.shape[2]
    side = tensor_blocks.shape[4]
    full_a = factor_a.reshape(-1, width)
    full_b = factor_b.reshape(-1, width)
    full_c = factor_c.reshape(-1, width)
    gram_b = gram_rows(full_b)
    gram_c = gram_rows(full_c)

    def first_terms(block, starts):
        band_b = lax.dynamic_slice_in_dim(full_b, starts[1], side, 0)
        band_c = lax.dynamic_slice_in_dim(full_c, starts[2], side, 0)
        contracted = jnp.dot(block.reshape(side * side, side), band_c, preferred_element_type=jnp.float32).reshape(side, side, width)
        return starts[0], jnp.sum(contracted * band_b.astype(jnp.float32)[None], axis=1)

    sums_a = walk(tensor_blocks, block_coords, live_counts, jnp.zeros((full_a.shape[0], width), jnp.float32), first_terms)
    penalty, inverse = newton_inverse(gram_b, gram_c)
    new_a = split_updates(sums_a, full_a, penalty, inverse)
    gram_a = gram_rows(new_a)

    def project(block, starts):
        band_a = lax.dynamic_slice_in_dim(new_a, starts[0], side, 0)
        projected = lax.dot_general(band_a, block.reshape(side, side * side), (((0,), (0,)), ((), ())), preferred_element_type=jnp.float32)
        return projected.reshape(width, side, side)

    def second_terms(block, starts):
        band_c = lax.dynamic_slice_in_dim(full_c, starts[2], side, 0)
        projected = project(block, starts)
        return starts[1], jnp.sum(projected * band_c.astype(jnp.float32).T[:, None, :], axis=2).T

    sums_b = walk(tensor_blocks, block_coords, live_counts, jnp.zeros((full_b.shape[0], width), jnp.float32), second_terms)
    penalty, inverse = newton_inverse(gram_a, gram_c)
    new_b = split_updates(sums_b, full_b, penalty, inverse)
    gram_b_new = gram_rows(new_b)

    def third_terms(block, starts):
        band_b = lax.dynamic_slice_in_dim(new_b, starts[1], side, 0)
        projected = project(block, starts)
        return starts[2], jnp.sum(projected * band_b.astype(jnp.float32).T[:, :, None], axis=1).T

    sums_c = walk(tensor_blocks, block_coords, live_counts, jnp.zeros((full_c.shape[0], width), jnp.float32), third_terms)
    penalty, inverse = newton_inverse(gram_a, gram_b_new)
    new_c = split_updates(sums_c, full_c, penalty, inverse)
    return new_a.reshape(factor_a.shape), new_b.reshape(factor_b.shape), new_c.reshape(factor_c.shape)
```

```python
import functools

import jax
import jax.numpy as jnp
from jax import lax
from jax.experimental import pallas as pl
from jax.experimental.pallas import tpu as pltpu
from jax.sharding import PartitionSpec as P

NS_STEPS = 8
ADMM_ITERS = 4
SIDE = 128
WIDTH = 256
SLAB = 256
NX, NY, NZ = 16, 8, 2
NA = NY * NZ
NB = NX * NZ
F32 = jnp.float32
BF16 = jnp.bfloat16
MESH = pl.DeviceIdType.MESH
PHASES = 13
(B_ROWS, C_NEAR, C_ROWS, GB_PART, GB_ALL, A_SUMS, A_ROWS, GA_PART, GA_ALL, B_SUMS, B_NEW, GN_PART, GN_ALL) = range(PHASES)
C_SUMS, C_LAST = PHASES, PHASES + 1


def split(x):
    high = x.astype(BF16)
    return high, (x - high.astype(F32)).astype(BF16)


def dot(a, b):
    return jnp.dot(a, b, preferred_element_type=F32)


def dot_first(a, b):
    return lax.dot_general(a, b, (((0,), (0,)), ((), ())), preferred_element_type=F32)


def dot_split(a, b):
    return dot(a[0], b[0]) + (dot(a[0], b[1]) + dot(a[1], b[0]))


def newton_inverse(gram_left, gram_right, p_ref, q_ref):
    rows = lax.broadcasted_iota(jnp.int32, (WIDTH, WIDTH), 0)
    columns = lax.broadcasted_iota(jnp.int32, (WIDTH, WIDTH), 1)
    eye = rows == columns
    weighted = gram_left * gram_right
    diagonal = jnp.sum(jnp.where(eye, weighted, 0.0), axis=0, keepdims=True)
    penalty = jnp.sum(diagonal, axis=1, keepdims=True) / WIDTH
    system = weighted + jnp.where(eye, penalty, 0.0)
    bound = jnp.max(jnp.sum(jnp.abs(system), axis=0, keepdims=True), axis=1, keepdims=True)
    q = system / bound
    p_ref[...] = jnp.where(eye, 2.0, 0.0) - q
    halves = split(q)
    q_ref[...] = 2.0 * q - dot_split(halves, halves)

    def step(t, carry):
        q = q_ref[...]
        p = p_ref[...]
        right = split(q)
        p_ref[...] = 2.0 * p - dot_split(split(p), right)
        q_ref[...] = 2.0 * q - dot_split(right, right)
        return carry

    lax.fori_loop(0, NS_STEPS - 2, step, 0)
    p = p_ref[...]
    inverse = (2.0 * p - dot_split(split(p), split(q_ref[...]))) / bound
    return penalty, split(inverse)


def row_update(totals, start, penalty, inverse):
    primal = start
    dual = jnp.zeros_like(primal)
    for step in range(ADMM_ITERS):
        target = dot_split(split(totals + penalty * (primal + dual)), inverse)
        primal = jnp.maximum(target - dual, 0.0)
        dual = dual + primal - target
    return primal


def packed(x):
    count = x.shape[0] // 8
    left = x[:, :128].reshape(count, 8, 128)
    right = x[:, 128:].reshape(count, 8, 128)
    return jnp.concatenate([left, right], axis=1)


def unpacked(x):
    count = x.shape[0]
    left = x[:, :8, :].reshape(count * 8, 128)
    right = x[:, 8:, :].reshape(count * 8, 128)
    return jnp.concatenate([left, right], axis=1)


def kernel(
    coords, live, x_hbm, own_a, own_b, own_c, out_a, out_b, out_c,
    x, stored, slab_b, slab_b32, slab_c, near_c, band_b, band_c, band_a, sums, terms,
    gram_own, gram_part, gram_b, gram_c, gram_a, gram_n, parts_a, parts_n,
    take_a, slab_a, take_b, new_b, take_c, last_c, p_ref, q_ref,
    x_sem, send_sem, recv_sem,
):
    gx, gy, gz = lax.axis_index("gx"), lax.axis_index("gy"), lax.axis_index("gz")
    at_a = gy * NZ + gz
    at_b = gx * NZ + gz

    def peer_a(d):
        other = lax.rem(at_a + d, NA)
        return (gx, lax.div(other, NZ), lax.rem(other, NZ))

    def peer_b(d):
        other = lax.rem(at_b + d, NB)
        return (lax.div(other, NZ), gy, lax.rem(other, NZ))

    def peer_x(d):
        return (lax.rem(gx + d, NX), gy, gz)

    def peer_y(d):
        return (gx, lax.rem(gy + d, NY), gz)

    def send(phase, count, peer, source, target):
        def one(d, carry):
            pltpu.make_async_remote_copy(
                src_ref=source(d), dst_ref=target(d), send_sem=send_sem.at[phase],
                recv_sem=recv_sem.at[phase], device_id=peer(d), device_id_type=MESH,
            ).start()
            return carry

        lax.fori_loop(1, count, one, 0)

    def received(phase, ref):
        pltpu.make_async_copy(ref, ref, recv_sem.at[phase]).wait()

    def sent(phase, ref):
        pltpu.make_async_copy(ref, ref, send_sem.at[phase]).wait()

    loads = [pltpu.make_async_copy(x_hbm.at[0, 0, 0, s], x.at[s], x_sem.at[s]) for s in range(2)]
    for load in loads:
        load.start()

    barrier = pltpu.get_barrier_semaphore()

    def greet(peer):
        def one(d, carry):
            pl.semaphore_signal(barrier, inc=1, device_id=peer(d), device_id_type=MESH)
            return carry

        return one

    lax.fori_loop(1, NB, greet(peer_b), 0)
    lax.fori_loop(1, NA, greet(peer_a), 0)

    slab_b[at_b] = packed(own_b[0].astype(F32))[0].astype(BF16)
    rows_c = own_c[0].astype(F32)
    lines = lax.broadcasted_iota(jnp.int32, (16, WIDTH), 0)
    mine_c = lax.div(lines, 2) == gy
    placed = jnp.where(mine_c, jnp.where(lax.rem(lines, 2) == 0, rows_c[0:1], rows_c[1:2]), 0.0)
    near_c[NY - 1] = placed.astype(BF16)
    flags = [[coords[s * 3 + m].astype(F32) for m in range(3)] for s in range(2)]
    alive = [(s < live[0]).astype(jnp.int32).astype(F32) for s in range(2)]

    pl.semaphore_wait(barrier, NA + NB - 2)

    def banded(slot, mode, ref, offset):
        flag = flags[slot][mode]
        low = ref[offset : offset + SIDE, :].astype(F32)
        high = ref[offset + SIDE : offset + 2 * SIDE, :].astype(F32)
        return low * (1.0 - flag) + high * flag

    send(B_ROWS, NB, peer_b, lambda d: slab_b.at[at_b], lambda d: slab_b.at[at_b])
    send(C_NEAR, NY, peer_y, lambda d: near_c.at[NY - 1], lambda d: near_c.at[d - 1])
    received(C_NEAR, near_c.at[pl.ds(0, NY - 1)])
    sixteen_c = jnp.sum(near_c[...].astype(F32), axis=0)
    row_c = pl.multiple_of(gz * SLAB + gx * 16, 16)
    slab_c[pl.ds(row_c, 16), :] = sixteen_c.astype(BF16)
    send(C_ROWS, NB, peer_b, lambda d: slab_c.at[pl.ds(row_c, 16)], lambda d: slab_c.at[pl.ds(row_c, 16)])

    received(B_ROWS, slab_b.at[pl.ds(0, NB - 1)])
    wide_b = unpacked(slab_b[...].astype(F32))
    slab_b32[...] = wide_b
    narrow_b = wide_b.astype(BF16)
    gram_own[0] = dot_first(narrow_b, narrow_b)
    row_b = pl.multiple_of(at_b * 8, 8)
    send(GB_PART, NY, peer_y, lambda d: gram_own.at[0, pl.ds(row_b, 8)], lambda d: gram_part.at[d - 1])
    for s in range(2):
        band_b[s] = banded(s, 1, slab_b32, 0)

    received(C_ROWS, slab_c.at[pl.ds(0, (NB - 1) * 16)])
    whole_c = slab_c[...]
    gram_c[...] = dot_first(whole_c, whole_c)
    slab_of_c = slab_c[pl.ds(pl.multiple_of(gz * SLAB, SLAB), SLAB), :].astype(F32)
    for s in range(2):
        flag = flags[s][2]
        band_c[s] = (slab_of_c[:SIDE] * (1.0 - flag) + slab_of_c[SIDE:] * flag).astype(BF16)

    received(GB_PART, gram_part)
    gram_b[pl.ds(row_b, 8), :] = gram_own[0, pl.ds(row_b, 8), :] + jnp.sum(gram_part[...], axis=0)
    send(GB_ALL, NB, peer_b, lambda d: gram_b.at[pl.ds(row_b, 8)], lambda d: gram_b.at[pl.ds(row_b, 8)])

    for load in loads:
        load.wait()
    for s in range(2):
        right = band_c[s]

        def first(g, carry, s=s, right=right):
            for h in range(2):
                at = g * 8 + h * 4
                left = x[s, pl.ds(at, 4)].reshape(4 * SIDE, SIDE)
                product = dot(left, right).reshape(4, SIDE, WIDTH)
                stored[s, pl.ds(at, 4)] = product
                weighted = jnp.sum(product * band_b[s][None], axis=1)
                for k in range(4):
                    terms[s, pl.ds(at + k, 1), :] = weighted[k : k + 1]
            return carry

        lax.fori_loop(0, SIDE // 8, first, 0)

    def gathered(mode):
        halves = []
        for h in range(2):
            total = jnp.zeros((SIDE, WIDTH), F32)
            for s in range(2):
                flag = flags[s][mode]
                weight = alive[s] * (flag if h else 1.0 - flag)
                total = total + terms[s] * weight
            halves.append(total)
        return halves

    for h, total in enumerate(gathered(0)):
        sums[0, h * SIDE : (h + 1) * SIDE, :] = total

    def rows_for(mode, owner, count):
        return sums.at[mode, pl.ds(pl.multiple_of(owner * count, count), count)]

    send(A_SUMS, NA, peer_a, lambda d: rows_for(0, lax.rem(at_a + d, NA), 16), lambda d: take_a.at[d - 1])

    received(GB_ALL, gram_b.at[pl.ds(0, (NB - 1) * 8)])
    penalty, inverse = newton_inverse(gram_b[...], gram_c[...], p_ref, q_ref)
    received(A_SUMS, take_a)
    row_a = pl.multiple_of(at_a * 16, 16)
    totals = sums[0, pl.ds(row_a, 16), :] + jnp.sum(take_a[...], axis=0)
    updated = row_update(totals, own_a[0].astype(F32), penalty, inverse).astype(BF16)
    out_a[0] = updated
    slab_a[pl.ds(row_a, 16), :] = updated
    send(A_ROWS, NA, peer_a, lambda d: slab_a.at[pl.ds(row_a, 16)], lambda d: slab_a.at[pl.ds(row_a, 16)])

    received(A_ROWS, slab_a.at[pl.ds(0, (NA - 1) * 16)])
    narrow_a = slab_a[...]
    gram_own[1] = dot_first(narrow_a, narrow_a)
    send(GA_PART, NX, peer_x, lambda d: gram_own.at[1, pl.ds(row_a, 16)], lambda d: parts_a.at[d - 1])

    for s in range(2):
        band_a[s] = banded(s, 0, slab_a, 0)
    for s in range(2):

        def second(g, total, s=s):
            for k in range(8):
                total = total + stored[s, g * 8 + k] * band_a[s, pl.ds(g * 8 + k, 1), :]
            return total

        terms[s] = lax.fori_loop(0, SIDE // 8, second, jnp.zeros((SIDE, WIDTH), F32))
    for h, total in enumerate(gathered(1)):
        sums[1, h * SIDE : (h + 1) * SIDE, :] = total
    send(B_SUMS, NB, peer_b, lambda d: rows_for(1, lax.rem(at_b + d, NB), 8), lambda d: take_b.at[d - 1])

    received(GA_PART, parts_a)
    gram_a[pl.ds(row_a, 16), :] = gram_own[1, pl.ds(row_a, 16), :] + jnp.sum(parts_a[...], axis=0)
    send(GA_ALL, NA, peer_a, lambda d: gram_a.at[pl.ds(row_a, 16)], lambda d: gram_a.at[pl.ds(row_a, 16)])
    received(GA_ALL, gram_a.at[pl.ds(0, (NA - 1) * 16)])

    penalty, inverse = newton_inverse(gram_a[...], gram_c[...], p_ref, q_ref)
    received(B_SUMS, take_b)
    totals = sums[1, pl.ds(row_b, 8), :] + jnp.sum(take_b[...], axis=0)
    updated = row_update(totals, own_b[0].astype(F32), penalty, inverse)
    out_b[0] = updated.astype(BF16)
    new_b[at_b] = packed(updated)[0].astype(BF16)
    send(B_NEW, NB, peer_b, lambda d: new_b.at[at_b], lambda d: new_b.at[at_b])

    received(B_NEW, new_b.at[pl.ds(0, NB - 1)])
    wide_b = unpacked(new_b[...].astype(F32))
    slab_b32[...] = wide_b
    narrow_b = wide_b.astype(BF16)
    gram_own[2] = dot_first(narrow_b, narrow_b)
    send(GN_PART, NY, peer_y, lambda d: gram_own.at[2, pl.ds(row_b, 8)], lambda d: parts_n.at[d - 1])

    for s in range(2):
        right = banded(s, 1, slab_b32, 0).astype(BF16)

        def third(g, total, s=s, right=right):
            for k in range(4):
                total = total + dot_first(x[s, g * 4 + k], right) * band_a[s, pl.ds(g * 4 + k, 1), :]
            return total

        terms[s] = lax.fori_loop(0, SIDE // 4, third, jnp.zeros((SIDE, WIDTH), F32))
        if s == 0:
            received(GN_PART, parts_n)
            gram_n[pl.ds(row_b, 8), :] = gram_own[2, pl.ds(row_b, 8), :] + jnp.sum(parts_n[...], axis=0)
            send(GN_ALL, NB, peer_b, lambda d: gram_n.at[pl.ds(row_b, 8)], lambda d: gram_n.at[pl.ds(row_b, 8)])
    for h, total in enumerate(gathered(2)):
        sums[2, h * SIDE : (h + 1) * SIDE, :] = total
    send(C_SUMS, NX, peer_x, lambda d: rows_for(2, lax.rem(gx + d, NX), 16), lambda d: take_c.at[d - 1])
    received(C_SUMS, take_c)
    here = pl.multiple_of(gx * 16, 16)
    last_c[NY - 1] = sums[2, pl.ds(here, 16), :] + jnp.sum(take_c[...], axis=0)
    send(C_LAST, NY, peer_y, lambda d: last_c.at[NY - 1], lambda d: last_c.at[d - 1])

    received(GN_ALL, gram_n.at[pl.ds(0, (NB - 1) * 8)])
    penalty, inverse = newton_inverse(gram_a[...], gram_n[...], p_ref, q_ref)
    received(C_LAST, last_c.at[pl.ds(0, NY - 1)])
    totals = jnp.sum(last_c[...], axis=0)
    start = slab_c[pl.ds(row_c, 16), :].astype(F32)
    updated = row_update(totals, start, penalty, inverse)
    chosen = [
        jnp.sum(jnp.where(lines == 2 * gy + k, updated, 0.0), axis=0, keepdims=True) for k in range(2)
    ]
    out_c[0] = jnp.concatenate(chosen, axis=0).astype(BF16)

    sent(B_ROWS, slab_b.at[pl.ds(0, NB - 1)])
    sent(C_NEAR, near_c.at[pl.ds(0, NY - 1)])
    sent(C_ROWS, slab_c.at[pl.ds(0, (NB - 1) * 16)])
    sent(GB_PART, gram_part)
    sent(GB_ALL, gram_b.at[pl.ds(0, (NB - 1) * 8)])
    sent(A_SUMS, take_a)
    sent(A_ROWS, slab_a.at[pl.ds(0, (NA - 1) * 16)])
    sent(GA_PART, parts_a)
    sent(GA_ALL, gram_a.at[pl.ds(0, (NA - 1) * 16)])
    sent(B_SUMS, take_b)
    sent(B_NEW, new_b.at[pl.ds(0, NB - 1)])
    sent(GN_PART, parts_n)
    sent(GN_ALL, gram_n.at[pl.ds(0, (NB - 1) * 8)])
    sent(C_SUMS, take_c)
    sent(C_LAST, last_c.at[pl.ds(0, NY - 1)])


def on_device(tensor_blocks, block_coords, live_counts, factor_a, factor_b, factor_c):
    vmem = pl.BlockSpec(memory_space=pltpu.VMEM)
    smem = pl.BlockSpec(memory_space=pltpu.SMEM)
    square = pltpu.VMEM((WIDTH, WIDTH), F32)
    scratch = [
        pltpu.VMEM((2, SIDE, SIDE, SIDE), BF16),
        pltpu.VMEM((2, SIDE, SIDE, WIDTH), F32),
        pltpu.VMEM((NB, 16, 128), BF16),
        square,
        pltpu.VMEM((NZ * SLAB, WIDTH), BF16),
        pltpu.VMEM((NY, 16, WIDTH), BF16),
        pltpu.VMEM((2, SIDE, WIDTH), F32),
        pltpu.VMEM((2, SIDE, WIDTH), BF16),
        pltpu.VMEM((2, SIDE, WIDTH), F32),
        pltpu.VMEM((3, SLAB, WIDTH), F32),
        pltpu.VMEM((2, SIDE, WIDTH), F32),
        pltpu.VMEM((3, WIDTH, WIDTH), F32),
        pltpu.VMEM((NY - 1, 8, WIDTH), F32),
        square,
        square,
        square,
        square,
        pltpu.VMEM((NX - 1, 16, WIDTH), F32),
        pltpu.VMEM((NY - 1, 8, WIDTH), F32),
        pltpu.VMEM((NA - 1, 16, WIDTH), F32),
        pltpu.VMEM((SLAB, WIDTH), BF16),
        pltpu.VMEM((NB - 1, 8, WIDTH), F32),
        pltpu.VMEM((NB, 16, 128), BF16),
        pltpu.VMEM((NX - 1, 16, WIDTH), F32),
        pltpu.VMEM((NY, 16, WIDTH), F32),
        square,
        square,
        pltpu.SemaphoreType.DMA((2,)),
        pltpu.SemaphoreType.DMA((PHASES + 2,)),
        pltpu.SemaphoreType.DMA((PHASES + 2,)),
    ]
    return pl.pallas_call(
        kernel,
        out_shape=(
            jax.ShapeDtypeStruct(factor_a.shape, BF16),
            jax.ShapeDtypeStruct(factor_b.shape, BF16),
            jax.ShapeDtypeStruct(factor_c.shape, BF16),
        ),
        in_specs=[smem, smem, pl.BlockSpec(memory_space=pl.ANY), vmem, vmem, vmem],
        out_specs=(vmem, vmem, vmem),
        scratch_shapes=scratch,
        compiler_params=pltpu.CompilerParams(
            collective_id=0, has_side_effects=True, vmem_limit_bytes=56 * 1024 * 1024
        ),
        name="sweep",
    )(block_coords.reshape(-1), live_counts.reshape(-1), tensor_blocks, factor_a, factor_b, factor_c)


def solution(mesh):
    factors = (P("gx", ("gy", "gz"), None), P("gy", ("gx", "gz"), None), P("gz", ("gx", "gy"), None))
    return jax.shard_map(
        on_device,
        mesh=mesh,
        in_specs=(P("gx", "gy", "gz"), P("gx", "gy", "gz"), P("gx", "gy", "gz"), *factors),
        out_specs=factors,
        check_vma=False,
    )
```

```python
import functools

import jax
import jax.numpy as jnp
from jax import lax
from jax.experimental import pallas as pl
from jax.experimental.pallas import tpu as pltpu
from jax.sharding import PartitionSpec as P

NS_STEPS = 8
ADMM_ITERS = 4
SIDE = 128
WIDTH = 256
SLAB = 256
NX, NY, NZ = 16, 8, 2
NA = NY * NZ
NB = NX * NZ
F32 = jnp.float32
BF16 = jnp.bfloat16
MESH = pl.DeviceIdType.MESH
PHASES = 13
(B_ROWS, C_NEAR, C_ROWS, GB_PART, GB_ALL, A_SUMS, A_ROWS, GA_PART, GA_ALL, B_SUMS, B_NEW, GN_PART, GN_ALL) = range(PHASES)
C_SUMS, C_LAST, C_OTHER = PHASES, PHASES + 1, PHASES + 2


def split(x):
    high = x.astype(BF16)
    return high, (x - high.astype(F32)).astype(BF16)


def dot(a, b):
    return jnp.dot(a, b, preferred_element_type=F32)


def dot_first(a, b):
    return lax.dot_general(a, b, (((0,), (0,)), ((), ())), preferred_element_type=F32)


def dot_split(a, b):
    return dot(a[0], b[0]) + (dot(a[0], b[1]) + dot(a[1], b[0]))


def newton_inverse(gram_left, gram_right, p_ref, q_ref):
    rows = lax.broadcasted_iota(jnp.int32, (WIDTH, WIDTH), 0)
    columns = lax.broadcasted_iota(jnp.int32, (WIDTH, WIDTH), 1)
    eye = rows == columns
    weighted = gram_left * gram_right
    diagonal = jnp.sum(jnp.where(eye, weighted, 0.0), axis=0, keepdims=True)
    penalty = jnp.sum(diagonal, axis=1, keepdims=True) / WIDTH
    system = weighted + jnp.where(eye, penalty, 0.0)
    bound = jnp.max(jnp.sum(jnp.abs(system), axis=0, keepdims=True), axis=1, keepdims=True)
    q = system / bound
    p_ref[...] = jnp.where(eye, 2.0, 0.0) - q
    halves = split(q)
    q_ref[...] = 2.0 * q - dot_split(halves, halves)

    def step(t, carry):
        q = q_ref[...]
        p = p_ref[...]
        right = split(q)
        p_ref[...] = 2.0 * p - dot_split(split(p), right)
        q_ref[...] = 2.0 * q - dot_split(right, right)
        return carry

    lax.fori_loop(0, NS_STEPS - 2, step, 0)
    p = p_ref[...]
    inverse = (2.0 * p - dot_split(split(p), split(q_ref[...]))) / bound
    return penalty, split(inverse)


def row_update(totals, start, penalty, inverse):
    primal = start
    dual = jnp.zeros_like(primal)
    for step in range(ADMM_ITERS):
        target = dot_split(split(totals + penalty * (primal + dual)), inverse)
        primal = jnp.maximum(target - dual, 0.0)
        dual = dual + primal - target
    return primal


def packed(x):
    count = x.shape[0] // 8
    left = x[:, :128].reshape(count, 8, 128)
    right = x[:, 128:].reshape(count, 8, 128)
    return jnp.concatenate([left, right], axis=1)


def unpacked(x):
    count = x.shape[0]
    left = x[:, :8, :].reshape(count * 8, 128)
    right = x[:, 8:, :].reshape(count * 8, 128)
    return jnp.concatenate([left, right], axis=1)


def kernel(
    coords, live, x_hbm, own_a, own_b, own_c, out_a, out_b, out_c,
    x, turned, stored, slab_b, slab_b32, slab_c, near_c, band_b, band_c, band_a, sums, terms,
    gram_own, gram_part, gram_b, gram_c, gram_a, gram_n, parts_a, parts_n,
    take_a, slab_a, take_b, new_b, take_c, last_c, p_ref, q_ref,
    x_sem, send_sem, recv_sem,
):
    gx, gy, gz = lax.axis_index("gx"), lax.axis_index("gy"), lax.axis_index("gz")
    at_a = gy * NZ + gz
    at_b = gx * NZ + gz

    def peer_a(d):
        other = lax.rem(at_a + d, NA)
        return (gx, lax.div(other, NZ), lax.rem(other, NZ))

    def peer_b(d):
        other = lax.rem(at_b + d, NB)
        return (lax.div(other, NZ), gy, lax.rem(other, NZ))

    def peer_x(d):
        return (lax.rem(gx + d, NX), gy, gz)

    def peer_z(d):
        return (gx, gy, lax.rem(gz + d, NZ))

    def peer_y(d):
        return (gx, lax.rem(gy + d, NY), gz)

    def send(phase, count, peer, source, target):
        def one(d, carry):
            pltpu.make_async_remote_copy(
                src_ref=source(d), dst_ref=target(d), send_sem=send_sem.at[phase],
                recv_sem=recv_sem.at[phase], device_id=peer(d), device_id_type=MESH,
            ).start()
            return carry

        lax.fori_loop(1, count, one, 0)

    def received(phase, ref):
        pltpu.make_async_copy(ref, ref, recv_sem.at[phase]).wait()

    def sent(phase, ref):
        pltpu.make_async_copy(ref, ref, send_sem.at[phase]).wait()

    loads = [pltpu.make_async_copy(x_hbm.at[0, 0, 0, s], x.at[s], x_sem.at[s]) for s in range(2)]
    for load in loads:
        load.start()

    barrier = pltpu.get_barrier_semaphore()

    def greet(peer):
        def one(d, carry):
            pl.semaphore_signal(barrier, inc=1, device_id=peer(d), device_id_type=MESH)
            return carry

        return one

    lax.fori_loop(1, NB, greet(peer_b), 0)
    lax.fori_loop(1, NA, greet(peer_a), 0)

    slab_b[at_b] = packed(own_b[0].astype(F32))[0].astype(BF16)
    rows_c = own_c[0].astype(F32)
    lines = lax.broadcasted_iota(jnp.int32, (16, WIDTH), 0)
    mine_c = lax.div(lines, 2) == gy
    placed = jnp.where(mine_c, jnp.where(lax.rem(lines, 2) == 0, rows_c[0:1], rows_c[1:2]), 0.0)
    near_c[NY - 1] = placed.astype(BF16)
    flags = [[coords[0, 0, 0, s, m].astype(F32) for m in range(3)] for s in range(2)]
    alive = [(live[0] > s).astype(jnp.int32).astype(F32) for s in range(2)]

    def turn(s):
        loads[s].wait()

        def one(g, carry):
            at = pl.multiple_of(g * 16, 16)
            turned[s, :, pl.ds(at, 16), :] = jnp.swapaxes(x[s, pl.ds(at, 16)], 0, 1)
            return carry

        lax.fori_loop(0, SIDE // 16, one, 0)

    turn(0)
    pl.semaphore_wait(barrier, NA + NB - 2)

    def banded(slot, mode, ref, offset):
        flag = flags[slot][mode]
        low = ref[offset : offset + SIDE, :].astype(F32)
        high = ref[offset + SIDE : offset + 2 * SIDE, :].astype(F32)
        return low * (1.0 - flag) + high * flag

    send(B_ROWS, NB, peer_b, lambda d: slab_b.at[at_b], lambda d: slab_b.at[at_b])
    send(C_NEAR, NY, peer_y, lambda d: near_c.at[NY - 1], lambda d: near_c.at[d - 1])
    turn(1)
    received(C_NEAR, near_c.at[pl.ds(0, NY - 1)])
    sixteen_c = jnp.sum(near_c[...].astype(F32), axis=0)
    row_c = pl.multiple_of(gz * SLAB + gx * 16, 16)
    slab_c[pl.ds(row_c, 16), :] = sixteen_c.astype(BF16)
    send(C_ROWS, NX, peer_x, lambda d: slab_c.at[pl.ds(row_c, 16)], lambda d: slab_c.at[pl.ds(row_c, 16)])

    received(B_ROWS, slab_b.at[pl.ds(0, NB - 1)])
    wide_b = unpacked(slab_b[...].astype(F32))
    slab_b32[...] = wide_b
    narrow_b = wide_b.astype(BF16)
    gram_own[0] = dot_first(narrow_b, narrow_b)
    row_b = pl.multiple_of(at_b * 8, 8)
    send(GB_PART, NY, peer_y, lambda d: gram_own.at[0, pl.ds(row_b, 8)], lambda d: gram_part.at[d - 1])
    for s in range(2):
        band_b[s] = banded(s, 1, slab_b32, 0)

    received(C_ROWS, slab_c.at[pl.ds(0, (NX - 1) * 16)])
    half_c = pl.ds(pl.multiple_of(gz * SLAB, SLAB), SLAB)
    send(C_OTHER, NZ, peer_z, lambda d: slab_c.at[half_c], lambda d: slab_c.at[half_c])
    slab_of_c = slab_c[half_c, :].astype(F32)
    for s in range(2):
        flag = flags[s][2]
        band_c[s] = (slab_of_c[:SIDE] * (1.0 - flag) + slab_of_c[SIDE:] * flag).astype(BF16)

    received(GB_PART, gram_part)
    gram_b[pl.ds(row_b, 8), :] = gram_own[0, pl.ds(row_b, 8), :] + jnp.sum(gram_part[...], axis=0)
    send(GB_ALL, NB, peer_b, lambda d: gram_b.at[pl.ds(row_b, 8)], lambda d: gram_b.at[pl.ds(row_b, 8)])

    for s in range(2):
        right = band_c[s]

        def first(g, carry, s=s, right=right):
            for h in range(4):
                at = pl.multiple_of(g * 32 + h * 8, 8)
                left = x[s, pl.ds(at, 8)].reshape(8 * SIDE, SIDE)
                product = dot(left, right).reshape(8, SIDE, WIDTH)
                stored[s, pl.ds(at, 8)] = product
                terms[s, pl.ds(at, 8), :] = jnp.sum(product * band_b[s][None], axis=1)
            return carry

        lax.fori_loop(0, SIDE // 32, first, 0)

    def gathered(mode):
        halves = []
        for h in range(2):
            total = jnp.zeros((SIDE, WIDTH), F32)
            for s in range(2):
                flag = flags[s][mode]
                weight = alive[s] * (flag if h else 1.0 - flag)
                total = total + terms[s] * weight
            halves.append(total)
        return halves

    for h, total in enumerate(gathered(0)):
        sums[0, h * SIDE : (h + 1) * SIDE, :] = total

    def rows_for(mode, owner, count):
        return sums.at[mode, pl.ds(pl.multiple_of(owner * count, count), count)]

    send(A_SUMS, NA, peer_a, lambda d: rows_for(0, lax.rem(at_a + d, NA), 16), lambda d: take_a.at[d - 1])

    received(C_OTHER, slab_c.at[half_c])
    whole_c = slab_c[...]
    gram_c[...] = dot_first(whole_c, whole_c)
    received(GB_ALL, gram_b.at[pl.ds(0, (NB - 1) * 8)])
    penalty, inverse = newton_inverse(gram_b[...], gram_c[...], p_ref, q_ref)
    received(A_SUMS, take_a)
    row_a = pl.multiple_of(at_a * 16, 16)
    totals = sums[0, pl.ds(row_a, 16), :] + jnp.sum(take_a[...], axis=0)
    updated = row_update(totals, own_a[0].astype(F32), penalty, inverse).astype(BF16)
    out_a[0] = updated
    slab_a[pl.ds(row_a, 16), :] = updated
    send(A_ROWS, NA, peer_a, lambda d: slab_a.at[pl.ds(row_a, 16)], lambda d: slab_a.at[pl.ds(row_a, 16)])

    received(A_ROWS, slab_a.at[pl.ds(0, (NA - 1) * 16)])
    narrow_a = slab_a[...]
    gram_own[1] = dot_first(narrow_a, narrow_a)
    send(GA_PART, NX, peer_x, lambda d: gram_own.at[1, pl.ds(row_a, 16)], lambda d: parts_a.at[d - 1])

    for s in range(2):
        band_a[s] = banded(s, 0, slab_a, 0)
    for s in range(2):

        def second(g, total, s=s):
            for k in range(8):
                total = total + stored[s, g * 8 + k] * band_a[s, pl.ds(g * 8 + k, 1), :]
            return total

        terms[s] = lax.fori_loop(0, SIDE // 8, second, jnp.zeros((SIDE, WIDTH), F32))
    for h, total in enumerate(gathered(1)):
        sums[1, h * SIDE : (h + 1) * SIDE, :] = total
    send(B_SUMS, NB, peer_b, lambda d: rows_for(1, lax.rem(at_b + d, NB), 8), lambda d: take_b.at[d - 1])

    def product_a(s):
        right = band_a[s].astype(BF16)

        def one(g, carry):
            for k in range(32):
                stored[s, g * 32 + k] = dot_first(turned[s, g * 32 + k], right)
            return carry

        lax.fori_loop(0, SIDE // 32, one, 0)

    product_a(0)

    received(GA_PART, parts_a)
    gram_a[pl.ds(row_a, 16), :] = gram_own[1, pl.ds(row_a, 16), :] + jnp.sum(parts_a[...], axis=0)
    send(GA_ALL, NA, peer_a, lambda d: gram_a.at[pl.ds(row_a, 16)], lambda d: gram_a.at[pl.ds(row_a, 16)])
    product_a(1)
    received(GA_ALL, gram_a.at[pl.ds(0, (NA - 1) * 16)])

    penalty, inverse = newton_inverse(gram_a[...], gram_c[...], p_ref, q_ref)
    received(B_SUMS, take_b)
    totals = sums[1, pl.ds(row_b, 8), :] + jnp.sum(take_b[...], axis=0)
    updated = row_update(totals, own_b[0].astype(F32), penalty, inverse)
    out_b[0] = updated.astype(BF16)
    new_b[at_b] = packed(updated)[0].astype(BF16)
    send(B_NEW, NB, peer_b, lambda d: new_b.at[at_b], lambda d: new_b.at[at_b])

    received(B_NEW, new_b.at[pl.ds(0, NB - 1)])
    wide_b = unpacked(new_b[...].astype(F32))
    slab_b32[...] = wide_b
    narrow_b = wide_b.astype(BF16)
    gram_own[2] = dot_first(narrow_b, narrow_b)
    send(GN_PART, NY, peer_y, lambda d: gram_own.at[2, pl.ds(row_b, 8)], lambda d: parts_n.at[d - 1])

    for s in range(2):
        band_b[s] = banded(s, 1, slab_b32, 0)
    for s in range(2):

        def third(g, total, s=s):
            for k in range(8):
                total = total + stored[s, g * 8 + k] * band_b[s, pl.ds(g * 8 + k, 1), :]
            return total

        terms[s] = lax.fori_loop(0, SIDE // 8, third, jnp.zeros((SIDE, WIDTH), F32))
    for h, total in enumerate(gathered(2)):
        sums[2, h * SIDE : (h + 1) * SIDE, :] = total
    send(C_SUMS, NX, peer_x, lambda d: rows_for(2, lax.rem(gx + d, NX), 16), lambda d: take_c.at[d - 1])

    received(GN_PART, parts_n)
    gram_n[pl.ds(row_b, 8), :] = gram_own[2, pl.ds(row_b, 8), :] + jnp.sum(parts_n[...], axis=0)
    send(GN_ALL, NB, peer_b, lambda d: gram_n.at[pl.ds(row_b, 8)], lambda d: gram_n.at[pl.ds(row_b, 8)])
    received(C_SUMS, take_c)
    here = pl.multiple_of(gx * 16, 16)
    last_c[NY - 1] = sums[2, pl.ds(here, 16), :] + jnp.sum(take_c[...], axis=0)
    send(C_LAST, NY, peer_y, lambda d: last_c.at[NY - 1], lambda d: last_c.at[d - 1])

    received(GN_ALL, gram_n.at[pl.ds(0, (NB - 1) * 8)])
    penalty, inverse = newton_inverse(gram_a[...], gram_n[...], p_ref, q_ref)
    received(C_LAST, last_c.at[pl.ds(0, NY - 1)])
    totals = jnp.sum(last_c[...], axis=0)
    start = slab_c[pl.ds(row_c, 16), :].astype(F32)
    updated = row_update(totals, start, penalty, inverse)
    chosen = [
        jnp.sum(jnp.where(lines == 2 * gy + k, updated, 0.0), axis=0, keepdims=True) for k in range(2)
    ]
    out_c[0] = jnp.concatenate(chosen, axis=0).astype(BF16)

    sent(B_ROWS, slab_b.at[pl.ds(0, NB - 1)])
    sent(C_NEAR, near_c.at[pl.ds(0, NY - 1)])
    sent(C_ROWS, slab_c.at[pl.ds(0, (NX - 1) * 16)])
    sent(C_OTHER, slab_c.at[half_c])
    sent(GB_PART, gram_part)
    sent(GB_ALL, gram_b.at[pl.ds(0, (NB - 1) * 8)])
    sent(A_SUMS, take_a)
    sent(A_ROWS, slab_a.at[pl.ds(0, (NA - 1) * 16)])
    sent(GA_PART, parts_a)
    sent(GA_ALL, gram_a.at[pl.ds(0, (NA - 1) * 16)])
    sent(B_SUMS, take_b)
    sent(B_NEW, new_b.at[pl.ds(0, NB - 1)])
    sent(GN_PART, parts_n)
    sent(GN_ALL, gram_n.at[pl.ds(0, (NB - 1) * 8)])
    sent(C_SUMS, take_c)
    sent(C_LAST, last_c.at[pl.ds(0, NY - 1)])


def hand_over(in_a, in_b, in_c, out_a, out_b, out_c):
    out_a[...] = in_a[...]
    out_b[...] = in_b[...]
    out_c[...] = in_c[...]


def on_device(tensor_blocks, block_coords, live_counts, factor_a, factor_b, factor_c):
    vmem = pl.BlockSpec(memory_space=pltpu.VMEM)
    smem = pl.BlockSpec(memory_space=pltpu.SMEM)
    square = pltpu.VMEM((WIDTH, WIDTH), F32)
    scratch = [
        pltpu.VMEM((2, SIDE, SIDE, SIDE), BF16),
        pltpu.VMEM((2, SIDE, SIDE, SIDE), BF16),
        pltpu.VMEM((2, SIDE, SIDE, WIDTH), F32),
        pltpu.VMEM((NB, 16, 128), BF16),
        square,
        pltpu.VMEM((NZ * SLAB, WIDTH), BF16),
        pltpu.VMEM((NY, 16, WIDTH), BF16),
        pltpu.VMEM((2, SIDE, WIDTH), F32),
        pltpu.VMEM((2, SIDE, WIDTH), BF16),
        pltpu.VMEM((2, SIDE, WIDTH), F32),
        pltpu.VMEM((3, SLAB, WIDTH), F32),
        pltpu.VMEM((2, SIDE, WIDTH), F32),
        pltpu.VMEM((3, WIDTH, WIDTH), F32),
        pltpu.VMEM((NY - 1, 8, WIDTH), F32),
        square,
        square,
        square,
        square,
        pltpu.VMEM((NX - 1, 16, WIDTH), F32),
        pltpu.VMEM((NY - 1, 8, WIDTH), F32),
        pltpu.VMEM((NA - 1, 16, WIDTH), F32),
        pltpu.VMEM((SLAB, WIDTH), BF16),
        pltpu.VMEM((NB - 1, 8, WIDTH), F32),
        pltpu.VMEM((NB, 16, 128), BF16),
        pltpu.VMEM((NX - 1, 16, WIDTH), F32),
        pltpu.VMEM((NY, 16, WIDTH), F32),
        square,
        square,
        pltpu.SemaphoreType.DMA((2,)),
        pltpu.SemaphoreType.DMA((PHASES + 3,)),
        pltpu.SemaphoreType.DMA((PHASES + 3,)),
    ]
    shapes = tuple(jax.ShapeDtypeStruct(f.shape, BF16) for f in (factor_a, factor_b, factor_c))
    updated = pl.pallas_call(
        kernel,
        out_shape=shapes,
        in_specs=[smem, vmem, pl.BlockSpec(memory_space=pl.ANY), vmem, vmem, vmem],
        out_specs=(vmem, vmem, vmem),
        scratch_shapes=scratch,
        compiler_params=pltpu.CompilerParams(
            collective_id=0, has_side_effects=True, vmem_limit_bytes=60 * 1024 * 1024
        ),
        name="sweep",
    )(block_coords, live_counts, tensor_blocks, factor_a, factor_b, factor_c)
    return pl.pallas_call(
        hand_over, out_shape=shapes, in_specs=[vmem] * 3, out_specs=(vmem,) * 3, name="hand_over"
    )(*updated)


def solution(mesh):
    factors = (P("gx", ("gy", "gz"), None), P("gy", ("gx", "gz"), None), P("gz", ("gx", "gy"), None))
    return jax.shard_map(
        on_device,
        mesh=mesh,
        in_specs=(P("gx", "gy", "gz"), P("gx", "gy", "gz"), P("gx", "gy", "gz"), *factors),
        out_specs=factors,
        check_vma=False,
    )
```

```python
import functools

import jax
import jax.numpy as jnp
from jax import lax
from jax.experimental import pallas as pl
from jax.experimental.pallas import tpu as pltpu
from jax.sharding import PartitionSpec as P

NS_STEPS = 8
ADMM_ITERS = 4
SIDE = 128
WIDTH = 256
SLAB = 256
NX, NY, NZ = 16, 8, 2
NA = NY * NZ
NB = NX * NZ
LINE = 4
NG = LINE * NZ
PIECE = WIDTH // NG
F32 = jnp.float32
BF16 = jnp.bfloat16
MESH = pl.DeviceIdType.MESH
PHASES = 13
(B_ROWS, C_NEAR, C_ROWS, GB_PART, GB_ALL, A_SUMS, A_ROWS, GA_PART, GA_ALL, B_SUMS, B_NEW, GN_PART, GN_ALL) = range(PHASES)
C_SUMS, C_LAST, C_OTHER = PHASES, PHASES + 1, PHASES + 2


def split(x):
    high = x.astype(BF16)
    return high, (x - high.astype(F32)).astype(BF16)


def dot(a, b):
    return jnp.dot(a, b, preferred_element_type=F32)


def dot_first(a, b):
    return lax.dot_general(a, b, (((0,), (0,)), ((), ())), preferred_element_type=F32)


def dot_split(a, b):
    return dot(a[0], b[0]) + (dot(a[0], b[1]) + dot(a[1], b[0]))


def newton_inverse(gram_left, gram_right, p_ref, q_ref):
    rows = lax.broadcasted_iota(jnp.int32, (WIDTH, WIDTH), 0)
    columns = lax.broadcasted_iota(jnp.int32, (WIDTH, WIDTH), 1)
    eye = rows == columns
    weighted = gram_left * gram_right
    diagonal = jnp.sum(jnp.where(eye, weighted, 0.0), axis=0, keepdims=True)
    penalty = jnp.sum(diagonal, axis=1, keepdims=True) / WIDTH
    system = weighted + jnp.where(eye, penalty, 0.0)
    bound = jnp.max(jnp.sum(jnp.abs(system), axis=0, keepdims=True), axis=1, keepdims=True)
    q = system / bound
    p_ref[...] = jnp.where(eye, 2.0, 0.0) - q
    halves = split(q)
    q_ref[...] = 2.0 * q - dot_split(halves, halves)

    def step(t, carry):
        q = q_ref[...]
        p = p_ref[...]
        right = split(q)
        p_ref[...] = 2.0 * p - dot_split(split(p), right)
        q_ref[...] = 2.0 * q - dot_split(right, right)
        return carry

    lax.fori_loop(0, NS_STEPS - 2, step, 0)
    p = p_ref[...]
    inverse = (2.0 * p - dot_split(split(p), split(q_ref[...]))) / bound
    return penalty, split(inverse)


def row_update(totals, start, penalty, inverse):
    primal = start
    dual = jnp.zeros_like(primal)
    for step in range(ADMM_ITERS):
        target = dot_split(split(totals + penalty * (primal + dual)), inverse)
        primal = jnp.maximum(target - dual, 0.0)
        dual = dual + primal - target
    return primal


def packed(x):
    count = x.shape[0] // 8
    left = x[:, :128].reshape(count, 8, 128)
    right = x[:, 128:].reshape(count, 8, 128)
    return jnp.concatenate([left, right], axis=1)


def unpacked(x):
    count = x.shape[0]
    left = x[:, :8, :].reshape(count * 8, 128)
    right = x[:, 8:, :].reshape(count * 8, 128)
    return jnp.concatenate([left, right], axis=1)


def kernel(
    coords, live, x_hbm, own_a, own_b, own_c, out_a, out_b, out_c,
    x, turned, stored, slab_b, slab_b32, slab_c, near_c, band_b, band_c, band_a, sums, terms,
    gram_own, gram_part, gram_b, gram_c, gram_a, gram_n, parts_a, parts_n,
    take_a, slab_a, take_b, new_b, take_c, last_c, p_ref, q_ref,
    x_sem, send_sem, recv_sem,
):
    gx, gy, gz = lax.axis_index("gx"), lax.axis_index("gy"), lax.axis_index("gz")
    at_a = gy * NZ + gz
    at_b = gx * NZ + gz

    def peer_a(d):
        other = lax.rem(at_a + d, NA)
        return (gx, lax.div(other, NZ), lax.rem(other, NZ))

    def peer_b(d):
        other = lax.rem(at_b + d, NB)
        return (lax.div(other, NZ), gy, lax.rem(other, NZ))

    at_g = lax.rem(gx, LINE) * NZ + gz

    def peer_g(d):
        other = lax.rem(at_g + d, NG)
        return (lax.div(gx, LINE) * LINE + lax.div(other, NZ), gy, lax.rem(other, NZ))

    def peer_x(d):
        return (lax.rem(gx + d, NX), gy, gz)

    def peer_z(d):
        return (gx, gy, lax.rem(gz + d, NZ))

    def peer_y(d):
        return (gx, lax.rem(gy + d, NY), gz)

    def send(phase, count, peer, source, target, when=None):
        def start(d):
            pltpu.make_async_remote_copy(
                src_ref=source(d), dst_ref=target(d), send_sem=send_sem.at[phase],
                recv_sem=recv_sem.at[phase], device_id=peer(d), device_id_type=MESH,
            ).start()

        def one(d, carry):
            if when is None:
                start(d)
            else:
                pl.when(when(d))(lambda: start(d))
            return carry

        lax.fori_loop(1, count, one, 0)

    def received(phase, ref):
        pltpu.make_async_copy(ref, ref, recv_sem.at[phase]).wait()

    def sent(phase, ref):
        pltpu.make_async_copy(ref, ref, send_sem.at[phase]).wait()

    loads = [pltpu.make_async_copy(x_hbm.at[0, 0, 0, s], x.at[s], x_sem.at[s]) for s in range(2)]
    for load in loads:
        load.start()

    barrier = pltpu.get_barrier_semaphore()

    def greet(peer):
        def one(d, carry):
            pl.semaphore_signal(barrier, inc=1, device_id=peer(d), device_id_type=MESH)
            return carry

        return one

    lax.fori_loop(1, NB, greet(peer_b), 0)
    lax.fori_loop(1, NA, greet(peer_a), 0)

    slab_b[at_b] = packed(own_b[0].astype(F32))[0].astype(BF16)
    rows_c = own_c[0].astype(F32)
    lines = lax.broadcasted_iota(jnp.int32, (16, WIDTH), 0)
    mine_c = lax.div(lines, 2) == gy
    placed = jnp.where(mine_c, jnp.where(lax.rem(lines, 2) == 0, rows_c[0:1], rows_c[1:2]), 0.0)
    near_c[NY - 1] = placed.astype(BF16)
    flags = [[coords[0, 0, 0, s, m].astype(F32) for m in range(3)] for s in range(2)]
    alive = [(live[0] > s).astype(jnp.int32).astype(F32) for s in range(2)]

    def turn(s):
        loads[s].wait()

        def one(g, carry):
            at = pl.multiple_of(g * 16, 16)
            turned[s, :, pl.ds(at, 16), :] = jnp.swapaxes(x[s, pl.ds(at, 16)], 0, 1)
            return carry

        lax.fori_loop(0, SIDE // 16, one, 0)

    pl.semaphore_wait(barrier, NA + NB - 2)

    def banded(slot, mode, ref, offset):
        flag = flags[slot][mode]
        low = ref[offset : offset + SIDE, :].astype(F32)
        high = ref[offset + SIDE : offset + 2 * SIDE, :].astype(F32)
        return low * (1.0 - flag) + high * flag

    send(C_NEAR, NY, peer_y, lambda d: near_c.at[NY - 1], lambda d: near_c.at[d - 1])
    send(B_ROWS, NB, peer_b, lambda d: slab_b.at[at_b], lambda d: slab_b.at[at_b])
    turn(0)
    received(C_NEAR, near_c.at[pl.ds(0, NY - 1)])
    sixteen_c = jnp.sum(near_c[...].astype(F32), axis=0)
    row_c = pl.multiple_of(gz * SLAB + gx * 16, 16)
    slab_c[pl.ds(row_c, 16), :] = sixteen_c.astype(BF16)
    send(C_ROWS, NX, peer_x, lambda d: slab_c.at[pl.ds(row_c, 16)], lambda d: slab_c.at[pl.ds(row_c, 16)])

    turn(1)

    received(B_ROWS, slab_b.at[pl.ds(0, NB - 1)])
    wide_b = unpacked(slab_b[...].astype(F32))
    slab_b32[...] = wide_b
    narrow_b = wide_b.astype(BF16)
    gram_own[0] = dot_first(narrow_b, narrow_b)
    row_b = pl.multiple_of(at_b * 8, 8)
    piece = pl.ds(pl.multiple_of(at_g * PIECE, PIECE), PIECE)
    send(GB_PART, NY, peer_y, lambda d: gram_own.at[0, piece], lambda d: gram_part.at[d - 1])
    for s in range(2):
        band_b[s] = banded(s, 1, slab_b32, 0)

    received(C_ROWS, slab_c.at[pl.ds(0, (NX - 1) * 16)])
    half_c = pl.ds(pl.multiple_of(gz * SLAB, SLAB), SLAB)
    send(C_OTHER, NZ, peer_z, lambda d: slab_c.at[half_c], lambda d: slab_c.at[half_c])
    slab_of_c = slab_c[half_c, :].astype(F32)
    for s in range(2):
        flag = flags[s][2]
        band_c[s] = (slab_of_c[:SIDE] * (1.0 - flag) + slab_of_c[SIDE:] * flag).astype(BF16)

    received(GB_PART, gram_part)
    gram_b[piece, :] = gram_own[0, piece, :] + jnp.sum(gram_part[...], axis=0)
    send(GB_ALL, NG, peer_g, lambda d: gram_b.at[piece], lambda d: gram_b.at[piece])

    def gather(mode, start, count):
        for h in range(2):
            total = jnp.zeros((count, WIDTH), F32)
            for s in range(2):
                flag = flags[s][mode]
                weight = alive[s] * (flag if h else 1.0 - flag)
                total = total + terms[s, start : start + count, :] * weight
            sums[mode, h * SIDE + start : h * SIDE + start + count, :] = total

    def rows_for(mode, owner, count):
        return sums.at[mode, pl.ds(pl.multiple_of(owner * count, count), count)]

    def in_half(owner, half):
        return lax.div(lax.rem(owner, 8), 4) == half

    for half in range(2):
        for s in range(2):
            right = band_c[s]

            def first(g, carry, s=s, right=right, half=half):
                for h in range(4):
                    at = pl.multiple_of(half * 64 + g * 32 + h * 8, 8)
                    left = x[s, pl.ds(at, 8)].reshape(8 * SIDE, SIDE)
                    product = dot(left, right).reshape(8, SIDE, WIDTH)
                    stored[s, pl.ds(at, 8)] = product
                    terms[s, pl.ds(at, 8), :] = jnp.sum(product * band_b[s][None], axis=1)
                return carry

            lax.fori_loop(0, 2, first, 0)
        gather(0, half * 64, 64)
        send(
            A_SUMS, NA, peer_a, lambda d: rows_for(0, lax.rem(at_a + d, NA), 16), lambda d: take_a.at[d - 1],
            when=lambda d, half=half: in_half(lax.rem(at_a + d, NA), half),
        )

    received(C_OTHER, slab_c.at[half_c])
    whole_c = slab_c[...]
    gram_c[...] = dot_first(whole_c, whole_c)
    received(GB_ALL, gram_b.at[pl.ds(0, (NG - 1) * PIECE)])
    penalty, inverse = newton_inverse(gram_b[...], gram_c[...], p_ref, q_ref)
    received(A_SUMS, take_a)
    row_a = pl.multiple_of(at_a * 16, 16)
    totals = sums[0, pl.ds(row_a, 16), :] + jnp.sum(take_a[...], axis=0)
    updated = row_update(totals, own_a[0].astype(F32), penalty, inverse).astype(BF16)
    out_a[0] = updated
    slab_a[pl.ds(row_a, 16), :] = updated
    send(A_ROWS, NA, peer_a, lambda d: slab_a.at[pl.ds(row_a, 16)], lambda d: slab_a.at[pl.ds(row_a, 16)])

    received(A_ROWS, slab_a.at[pl.ds(0, (NA - 1) * 16)])
    narrow_a = slab_a[...]
    gram_own[1] = dot_first(narrow_a, narrow_a)
    send(GA_PART, NX, peer_x, lambda d: gram_own.at[1, pl.ds(row_a, 16)], lambda d: parts_a.at[d - 1])

    for s in range(2):
        band_a[s] = banded(s, 0, slab_a, 0)
    for s in range(2):

        def second(g, total, s=s):
            for k in range(8):
                total = total + stored[s, g * 8 + k] * band_a[s, pl.ds(g * 8 + k, 1), :]
            return total

        terms[s] = lax.fori_loop(0, SIDE // 8, second, jnp.zeros((SIDE, WIDTH), F32))
    gather(1, 0, SIDE)
    send(B_SUMS, NB, peer_b, lambda d: rows_for(1, lax.rem(at_b + d, NB), 8), lambda d: take_b.at[d - 1])

    def product_a(s):
        right = band_a[s].astype(BF16)

        def one(g, carry):
            for k in range(32):
                stored[s, g * 32 + k] = dot_first(turned[s, g * 32 + k], right)
            return carry

        lax.fori_loop(0, SIDE // 32, one, 0)

    product_a(0)

    received(GA_PART, parts_a)
    gram_a[pl.ds(row_a, 16), :] = gram_own[1, pl.ds(row_a, 16), :] + jnp.sum(parts_a[...], axis=0)
    send(GA_ALL, NA, peer_a, lambda d: gram_a.at[pl.ds(row_a, 16)], lambda d: gram_a.at[pl.ds(row_a, 16)])
    product_a(1)
    received(GA_ALL, gram_a.at[pl.ds(0, (NA - 1) * 16)])

    penalty, inverse = newton_inverse(gram_a[...], gram_c[...], p_ref, q_ref)
    received(B_SUMS, take_b)
    totals = sums[1, pl.ds(row_b, 8), :] + jnp.sum(take_b[...], axis=0)
    updated = row_update(totals, own_b[0].astype(F32), penalty, inverse)
    out_b[0] = updated.astype(BF16)
    new_b[at_b] = packed(updated)[0].astype(BF16)
    send(B_NEW, NB, peer_b, lambda d: new_b.at[at_b], lambda d: new_b.at[at_b])

    received(B_NEW, new_b.at[pl.ds(0, NB - 1)])
    wide_b = unpacked(new_b[...].astype(F32))
    slab_b32[...] = wide_b
    narrow_b = wide_b.astype(BF16)
    gram_own[2] = dot_first(narrow_b, narrow_b)
    send(GN_PART, NY, peer_y, lambda d: gram_own.at[2, piece], lambda d: parts_n.at[d - 1])

    for s in range(2):
        band_b[s] = banded(s, 1, slab_b32, 0)
    for half in range(2):
        for s in range(2):

            def third(g, total, s=s, half=half):
                for k in range(16):
                    total = total + stored[s, g * 16 + k, half * 64 : half * 64 + 64] * band_b[s, pl.ds(g * 16 + k, 1), :]
                return total

            terms[s, half * 64 : half * 64 + 64, :] = lax.fori_loop(
                0, SIDE // 16, third, jnp.zeros((64, WIDTH), F32)
            )
        gather(2, half * 64, 64)
        send(
            C_SUMS, NX, peer_x, lambda d: rows_for(2, lax.rem(gx + d, NX), 16), lambda d: take_c.at[d - 1],
            when=lambda d, half=half: in_half(lax.rem(gx + d, NX), half),
        )

    received(GN_PART, parts_n)
    gram_n[piece, :] = gram_own[2, piece, :] + jnp.sum(parts_n[...], axis=0)
    send(GN_ALL, NG, peer_g, lambda d: gram_n.at[piece], lambda d: gram_n.at[piece])
    received(C_SUMS, take_c)
    here = pl.multiple_of(gx * 16, 16)
    last_c[NY - 1] = sums[2, pl.ds(here, 16), :] + jnp.sum(take_c[...], axis=0)
    send(C_LAST, NY, peer_y, lambda d: last_c.at[NY - 1], lambda d: last_c.at[d - 1])

    received(GN_ALL, gram_n.at[pl.ds(0, (NG - 1) * PIECE)])
    penalty, inverse = newton_inverse(gram_a[...], gram_n[...], p_ref, q_ref)
    received(C_LAST, last_c.at[pl.ds(0, NY - 1)])
    totals = jnp.sum(last_c[...], axis=0)
    start = slab_c[pl.ds(row_c, 16), :].astype(F32)
    updated = row_update(totals, start, penalty, inverse)
    chosen = [
        jnp.sum(jnp.where(lines == 2 * gy + k, updated, 0.0), axis=0, keepdims=True) for k in range(2)
    ]
    out_c[0] = jnp.concatenate(chosen, axis=0).astype(BF16)

    sent(B_ROWS, slab_b.at[pl.ds(0, NB - 1)])
    sent(C_NEAR, near_c.at[pl.ds(0, NY - 1)])
    sent(C_ROWS, slab_c.at[pl.ds(0, (NX - 1) * 16)])
    sent(C_OTHER, slab_c.at[half_c])
    sent(GB_PART, gram_part)
    sent(GB_ALL, gram_b.at[pl.ds(0, (NG - 1) * PIECE)])
    sent(A_SUMS, take_a)
    sent(A_ROWS, slab_a.at[pl.ds(0, (NA - 1) * 16)])
    sent(GA_PART, parts_a)
    sent(GA_ALL, gram_a.at[pl.ds(0, (NA - 1) * 16)])
    sent(B_SUMS, take_b)
    sent(B_NEW, new_b.at[pl.ds(0, NB - 1)])
    sent(GN_PART, parts_n)
    sent(GN_ALL, gram_n.at[pl.ds(0, (NG - 1) * PIECE)])
    sent(C_SUMS, take_c)
    sent(C_LAST, last_c.at[pl.ds(0, NY - 1)])


def hand_over(in_a, in_b, in_c, out_a, out_b, out_c):
    out_a[...] = in_a[...]
    out_b[...] = in_b[...]
    out_c[...] = in_c[...]


def on_device(tensor_blocks, block_coords, live_counts, factor_a, factor_b, factor_c):
    vmem = pl.BlockSpec(memory_space=pltpu.VMEM)
    smem = pl.BlockSpec(memory_space=pltpu.SMEM)
    square = pltpu.VMEM((WIDTH, WIDTH), F32)
    scratch = [
        pltpu.VMEM((2, SIDE, SIDE, SIDE), BF16),
        pltpu.VMEM((2, SIDE, SIDE, SIDE), BF16),
        pltpu.VMEM((2, SIDE, SIDE, WIDTH), F32),
        pltpu.VMEM((NB, 16, 128), BF16),
        square,
        pltpu.VMEM((NZ * SLAB, WIDTH), BF16),
        pltpu.VMEM((NY, 16, WIDTH), BF16),
        pltpu.VMEM((2, SIDE, WIDTH), F32),
        pltpu.VMEM((2, SIDE, WIDTH), BF16),
        pltpu.VMEM((2, SIDE, WIDTH), F32),
        pltpu.VMEM((3, SLAB, WIDTH), F32),
        pltpu.VMEM((2, SIDE, WIDTH), F32),
        pltpu.VMEM((3, WIDTH, WIDTH), F32),
        pltpu.VMEM((NY - 1, PIECE, WIDTH), F32),
        square,
        square,
        square,
        square,
        pltpu.VMEM((NX - 1, 16, WIDTH), F32),
        pltpu.VMEM((NY - 1, PIECE, WIDTH), F32),
        pltpu.VMEM((NA - 1, 16, WIDTH), F32),
        pltpu.VMEM((SLAB, WIDTH), BF16),
        pltpu.VMEM((NB - 1, 8, WIDTH), F32),
        pltpu.VMEM((NB, 16, 128), BF16),
        pltpu.VMEM((NX - 1, 16, WIDTH), F32),
        pltpu.VMEM((NY, 16, WIDTH), F32),
        square,
        square,
        pltpu.SemaphoreType.DMA((2,)),
        pltpu.SemaphoreType.DMA((PHASES + 3,)),
        pltpu.SemaphoreType.DMA((PHASES + 3,)),
    ]
    shapes = tuple(jax.ShapeDtypeStruct(f.shape, BF16) for f in (factor_a, factor_b, factor_c))
    updated = pl.pallas_call(
        kernel,
        out_shape=shapes,
        in_specs=[smem, vmem, pl.BlockSpec(memory_space=pl.ANY), vmem, vmem, vmem],
        out_specs=(vmem, vmem, vmem),
        scratch_shapes=scratch,
        compiler_params=pltpu.CompilerParams(
            collective_id=0, has_side_effects=True, vmem_limit_bytes=60 * 1024 * 1024
        ),
        name="sweep",
    )(block_coords, live_counts, tensor_blocks, factor_a, factor_b, factor_c)
    return pl.pallas_call(
        hand_over, out_shape=shapes, in_specs=[vmem] * 3, out_specs=(vmem,) * 3, name="hand_over"
    )(*updated)


def solution(mesh):
    factors = (P("gx", ("gy", "gz"), None), P("gy", ("gx", "gz"), None), P("gz", ("gx", "gy"), None))
    return jax.shard_map(
        on_device,
        mesh=mesh,
        in_specs=(P("gx", "gy", "gz"), P("gx", "gy", "gz"), P("gx", "gy", "gz"), *factors),
        out_specs=factors,
        check_vma=False,
    )
```

```python
import functools

import jax
import jax.numpy as jnp
from jax import lax
from jax.experimental import pallas as pl
from jax.experimental.pallas import tpu as pltpu
from jax.sharding import PartitionSpec as P

NS_STEPS = 8
ADMM_ITERS = 4
SIDE = 128
WIDTH = 256
SLAB = 256
NX, NY, NZ = 16, 8, 2
NA = NY * NZ
NB = NX * NZ
LINE = 4
NG = LINE * NZ
PIECE = WIDTH // NG
F32 = jnp.float32
BF16 = jnp.bfloat16
MESH = pl.DeviceIdType.MESH
PHASES = 13
(B_ROWS, C_NEAR, C_ROWS, GB_PART, GB_ALL, A_SUMS, A_ROWS, GA_PART, GA_ALL, B_SUMS, B_NEW, GN_PART, GN_ALL) = range(PHASES)
C_SUMS, C_LAST, C_OTHER, GA_DIAG = PHASES, PHASES + 1, PHASES + 2, PHASES + 3


def split(x):
    high = x.astype(BF16)
    return high, (x - high.astype(F32)).astype(BF16)


def dot(a, b):
    return jnp.dot(a, b, preferred_element_type=F32)


def dot_first(a, b):
    return lax.dot_general(a, b, (((0,), (0,)), ((), ())), preferred_element_type=F32)


def dot_split(a, b):
    return dot(a[0], b[0]) + (dot(a[0], b[1]) + dot(a[1], b[0]))


def newton_inverse(gram_left, gram_right, p_ref, q_ref):
    rows = lax.broadcasted_iota(jnp.int32, (WIDTH, WIDTH), 0)
    columns = lax.broadcasted_iota(jnp.int32, (WIDTH, WIDTH), 1)
    eye = rows == columns
    weighted = gram_left * gram_right
    diagonal = jnp.sum(jnp.where(eye, weighted, 0.0), axis=0, keepdims=True)
    penalty = jnp.sum(diagonal, axis=1, keepdims=True) / WIDTH
    system = weighted + jnp.where(eye, penalty, 0.0)
    bound = jnp.max(jnp.sum(jnp.abs(system), axis=0, keepdims=True), axis=1, keepdims=True)
    q = system / bound
    p_ref[...] = jnp.where(eye, 2.0, 0.0) - q
    halves = split(q)
    q_ref[...] = 2.0 * q - dot_split(halves, halves)

    def step(t, carry):
        q = q_ref[...]
        p = p_ref[...]
        right = split(q)
        p_ref[...] = 2.0 * p - dot_split(split(p), right)
        q_ref[...] = 2.0 * q - dot_split(right, right)
        return carry

    lax.fori_loop(0, NS_STEPS - 2, step, 0)
    p = p_ref[...]
    inverse = (2.0 * p - dot_split(split(p), split(q_ref[...]))) / bound
    return penalty, split(inverse)


def row_update(totals, start, penalty, inverse):
    count = start.shape[0]
    primal = start
    dual = jnp.zeros_like(primal)
    for step in range(ADMM_ITERS):
        value = totals + penalty * (primal + dual)
        high = value.astype(BF16).astype(F32)
        both = dot(jnp.concatenate([high, value - high], axis=0).astype(BF16), inverse[0])
        target = both[:count] + (both[count:] + dot(high.astype(BF16), inverse[1]))
        primal = jnp.maximum(target - dual, 0.0)
        dual = dual + primal - target
    return primal


def packed(x):
    count = x.shape[0] // 8
    left = x[:, :128].reshape(count, 8, 128)
    right = x[:, 128:].reshape(count, 8, 128)
    return jnp.concatenate([left, right], axis=1)


def unpacked(x):
    count = x.shape[0]
    left = x[:, :8, :].reshape(count * 8, 128)
    right = x[:, 8:, :].reshape(count * 8, 128)
    return jnp.concatenate([left, right], axis=1)


def kernel(
    coords, live, x_hbm, own_a, own_b, own_c, out_a, out_b, out_c,
    x, turned, stored, slab_b, slab_b32, slab_c, near_c, band_b, band_c, band_a, sums, terms,
    gram_own, gram_part, gram_b, gram_c, gram_a, gram_n, parts_a, parts_n,
    halved_own, halved, diagonals,
    take_a, slab_a, take_b, new_b, take_c, last_c, p_ref, q_ref,
    x_sem, send_sem, recv_sem,
):
    gx, gy, gz = lax.axis_index("gx"), lax.axis_index("gy"), lax.axis_index("gz")
    at_a = gy * NZ + gz
    at_b = gx * NZ + gz

    def peer_a(d):
        other = lax.rem(at_a + d, NA)
        return (gx, lax.div(other, NZ), lax.rem(other, NZ))

    def peer_b(d):
        other = lax.rem(at_b + d, NB)
        return (lax.div(other, NZ), gy, lax.rem(other, NZ))

    at_g = lax.rem(gx, LINE) * NZ + gz

    def peer_g(d):
        other = lax.rem(at_g + d, NG)
        return (lax.div(gx, LINE) * LINE + lax.div(other, NZ), gy, lax.rem(other, NZ))

    def peer_x(d):
        return (lax.rem(gx + d, NX), gy, gz)

    def peer_z(d):
        return (gx, gy, lax.rem(gz + d, NZ))

    def peer_y(d):
        return (gx, lax.rem(gy + d, NY), gz)

    def send(phase, count, peer, source, target, when=None):
        def start(d):
            pltpu.make_async_remote_copy(
                src_ref=source(d), dst_ref=target(d), send_sem=send_sem.at[phase],
                recv_sem=recv_sem.at[phase], device_id=peer(d), device_id_type=MESH,
            ).start()

        def one(d, carry):
            if when is None:
                start(d)
            else:
                pl.when(when(d))(lambda: start(d))
            return carry

        lax.fori_loop(1, count, one, 0)

    def received(phase, ref):
        pltpu.make_async_copy(ref, ref, recv_sem.at[phase]).wait()

    def sent(phase, ref):
        pltpu.make_async_copy(ref, ref, send_sem.at[phase]).wait()

    loads = [pltpu.make_async_copy(x_hbm.at[0, 0, 0, s], x.at[s], x_sem.at[s]) for s in range(2)]
    for load in loads:
        load.start()

    barrier = pltpu.get_barrier_semaphore()

    def greet(peer):
        def one(d, carry):
            pl.semaphore_signal(barrier, inc=1, device_id=peer(d), device_id_type=MESH)
            return carry

        return one

    lax.fori_loop(1, NB, greet(peer_b), 0)
    lax.fori_loop(1, NA, greet(peer_a), 0)

    slab_b[at_b] = packed(own_b[0].astype(F32))[0].astype(BF16)
    rows_c = own_c[0].astype(F32)
    lines = lax.broadcasted_iota(jnp.int32, (16, WIDTH), 0)
    mine_c = lax.div(lines, 2) == gy
    placed = jnp.where(mine_c, jnp.where(lax.rem(lines, 2) == 0, rows_c[0:1], rows_c[1:2]), 0.0)
    near_c[NY - 1] = placed.astype(BF16)
    flags = [[coords[0, 0, 0, s, m].astype(F32) for m in range(3)] for s in range(2)]
    alive = [(live[0] > s).astype(jnp.int32).astype(F32) for s in range(2)]

    def turn(s):
        loads[s].wait()

        def one(g, carry):
            at = pl.multiple_of(g * 16, 16)
            turned[s, :, pl.ds(at, 16), :] = jnp.swapaxes(x[s, pl.ds(at, 16)], 0, 1)
            return carry

        lax.fori_loop(0, SIDE // 16, one, 0)

    pl.semaphore_wait(barrier, NA + NB - 2)

    def banded(slot, mode, ref, offset):
        flag = flags[slot][mode]
        low = ref[offset : offset + SIDE, :].astype(F32)
        high = ref[offset + SIDE : offset + 2 * SIDE, :].astype(F32)
        return low * (1.0 - flag) + high * flag

    send(C_NEAR, NY, peer_y, lambda d: near_c.at[NY - 1], lambda d: near_c.at[d - 1])
    send(B_ROWS, NB, peer_b, lambda d: slab_b.at[at_b], lambda d: slab_b.at[at_b])
    turn(0)
    received(C_NEAR, near_c.at[pl.ds(0, NY - 1)])
    sixteen_c = jnp.sum(near_c[...].astype(F32), axis=0)
    row_c = pl.multiple_of(gz * SLAB + gx * 16, 16)
    slab_c[pl.ds(row_c, 16), :] = sixteen_c.astype(BF16)
    send(C_ROWS, NX, peer_x, lambda d: slab_c.at[pl.ds(row_c, 16)], lambda d: slab_c.at[pl.ds(row_c, 16)])

    turn(1)

    received(B_ROWS, slab_b.at[pl.ds(0, NB - 1)])
    wide_b = unpacked(slab_b[...].astype(F32))
    slab_b32[...] = wide_b
    narrow_b = wide_b.astype(BF16)
    gram_own[0] = dot_first(narrow_b, narrow_b)
    row_b = pl.multiple_of(at_b * 8, 8)
    piece = pl.ds(pl.multiple_of(at_g * PIECE, PIECE), PIECE)
    send(GB_PART, NY, peer_y, lambda d: gram_own.at[0, piece], lambda d: gram_part.at[d - 1])
    for s in range(2):
        band_b[s] = banded(s, 1, slab_b32, 0)

    received(C_ROWS, slab_c.at[pl.ds(0, (NX - 1) * 16)])
    half_c = pl.ds(pl.multiple_of(gz * SLAB, SLAB), SLAB)
    send(C_OTHER, NZ, peer_z, lambda d: slab_c.at[half_c], lambda d: slab_c.at[half_c])
    slab_of_c = slab_c[half_c, :].astype(F32)
    for s in range(2):
        flag = flags[s][2]
        band_c[s] = (slab_of_c[:SIDE] * (1.0 - flag) + slab_of_c[SIDE:] * flag).astype(BF16)

    def gather(mode, start, count):
        for h in range(2):
            total = jnp.zeros((count, WIDTH), F32)
            for s in range(2):
                flag = flags[s][mode]
                weight = alive[s] * (flag if h else 1.0 - flag)
                total = total + terms[s, start : start + count, :] * weight
            sums[mode, h * SIDE + start : h * SIDE + start + count, :] = total

    def rows_for(mode, owner, count):
        return sums.at[mode, pl.ds(pl.multiple_of(owner * count, count), count)]

    def in_half(owner, half):
        return lax.div(lax.rem(owner, 8), 4) == half

    for half in range(2):
        for s in range(2):
            right = band_c[s]

            def first(g, carry, s=s, right=right, half=half):
                for h in range(4):
                    at = pl.multiple_of(half * 64 + g * 32 + h * 8, 8)
                    left = x[s, pl.ds(at, 8)].reshape(8 * SIDE, SIDE)
                    product = dot(left, right).reshape(8, SIDE, WIDTH)
                    stored[s, pl.ds(at, 8)] = product
                    terms[s, pl.ds(at, 8), :] = jnp.sum(product * band_b[s][None], axis=1)
                return carry

            lax.fori_loop(0, 2, first, 0)
            if half == 0 and s == 0:
                received(GB_PART, gram_part)
                gram_b[piece, :] = gram_own[0, piece, :] + jnp.sum(gram_part[...], axis=0)
                send(GB_ALL, NG, peer_g, lambda d: gram_b.at[piece], lambda d: gram_b.at[piece])
        gather(0, half * 64, 64)
        send(
            A_SUMS, NA, peer_a, lambda d: rows_for(0, lax.rem(at_a + d, NA), 16), lambda d: take_a.at[d - 1],
            when=lambda d, half=half: in_half(lax.rem(at_a + d, NA), half),
        )

    received(C_OTHER, slab_c.at[half_c])
    whole_c = slab_c[...]
    gram_c[...] = dot_first(whole_c, whole_c)
    received(GB_ALL, gram_b.at[pl.ds(0, (NG - 1) * PIECE)])
    penalty, inverse = newton_inverse(gram_b[...], gram_c[...], p_ref, q_ref)
    received(A_SUMS, take_a)
    row_a = pl.multiple_of(at_a * 16, 16)
    totals = sums[0, pl.ds(row_a, 16), :] + jnp.sum(take_a[...], axis=0)
    updated = row_update(totals, own_a[0].astype(F32), penalty, inverse).astype(BF16)
    out_a[0] = updated
    slab_a[pl.ds(row_a, 16), :] = updated
    send(A_ROWS, NA, peer_a, lambda d: slab_a.at[pl.ds(row_a, 16)], lambda d: slab_a.at[pl.ds(row_a, 16)])

    received(A_ROWS, slab_a.at[pl.ds(0, (NA - 1) * 16)])
    narrow_a = slab_a[...]
    whole = dot_first(narrow_a, narrow_a)
    across = lax.broadcasted_iota(jnp.int32, (128, 128), 1)
    down = lax.broadcasted_iota(jnp.int32, (128, 128), 0)
    last = whole[128:, 128:]
    mixed = jnp.where(across >= down, whole[:128, :128], last)
    halved_own[:, :8, :] = whole[:128, 128:].reshape(NA, 8, 128)
    halved_own[:, 8:, :] = mixed.reshape(NA, 8, 128)
    diagonal = jnp.sum(jnp.where(across == down, last, 0.0), axis=0, keepdims=True)
    diagonals[NX - 1] = jnp.broadcast_to(diagonal, (8, 128))
    send(GA_PART, NX, peer_x, lambda d: halved_own.at[at_a], lambda d: parts_a.at[d - 1])
    send(GA_DIAG, NX, peer_x, lambda d: diagonals.at[NX - 1], lambda d: diagonals.at[d - 1])

    for s in range(2):
        band_a[s] = banded(s, 0, slab_a, 0)
    for s in range(2):

        def second(g, total, s=s):
            for k in range(8):
                total = total + stored[s, g * 8 + k] * band_a[s, pl.ds(g * 8 + k, 1), :]
            return total

        terms[s] = lax.fori_loop(0, SIDE // 8, second, jnp.zeros((SIDE, WIDTH), F32))
    gather(1, 0, SIDE)
    send(B_SUMS, NB, peer_b, lambda d: rows_for(1, lax.rem(at_b + d, NB), 8), lambda d: take_b.at[d - 1])

    def product_a(s, start):
        right = band_a[s].astype(BF16)

        def one(g, carry):
            for k in range(32):
                at = start + g * 32 + k
                stored[s, at] = dot_first(turned[s, at], right)
            return carry

        lax.fori_loop(0, 2, one, 0)

    product_a(0, 0)

    received(GA_PART, parts_a)
    halved[at_a] = halved_own[at_a] + jnp.sum(parts_a[...], axis=0)
    send(GA_ALL, NA, peer_a, lambda d: halved.at[at_a], lambda d: halved.at[at_a])
    received(GA_DIAG, diagonals.at[pl.ds(0, NX - 1)])
    diagonal = jnp.sum(diagonals[...], axis=0)[:1]
    product_a(0, 64)
    received(GA_ALL, halved.at[pl.ds(0, NA - 1)])
    corner = halved[:, :8, :].reshape(128, 128)
    mixed = halved[:, 8:, :].reshape(128, 128)
    flipped = mixed.T
    gram_a[:128, :128] = jnp.where(across >= down, mixed, flipped)
    gram_a[:128, 128:] = corner
    gram_a[128:, :128] = corner.T
    gram_a[128:, 128:] = jnp.where(across < down, mixed, jnp.where(across > down, flipped, diagonal))

    penalty, inverse = newton_inverse(gram_a[...], gram_c[...], p_ref, q_ref)
    received(B_SUMS, take_b)
    totals = sums[1, pl.ds(row_b, 8), :] + jnp.sum(take_b[...], axis=0)
    updated = row_update(totals, own_b[0].astype(F32), penalty, inverse)
    out_b[0] = updated.astype(BF16)
    new_b[at_b] = packed(updated)[0].astype(BF16)
    send(B_NEW, NB, peer_b, lambda d: new_b.at[at_b], lambda d: new_b.at[at_b])
    product_a(1, 0)
    product_a(1, 64)

    received(B_NEW, new_b.at[pl.ds(0, NB - 1)])
    wide_b = unpacked(new_b[...].astype(F32))
    slab_b32[...] = wide_b
    narrow_b = wide_b.astype(BF16)
    gram_own[2] = dot_first(narrow_b, narrow_b)
    send(GN_PART, NY, peer_y, lambda d: gram_own.at[2, piece], lambda d: parts_n.at[d - 1])

    for s in range(2):
        band_b[s] = banded(s, 1, slab_b32, 0)
    for half in range(2):
        for s in range(2):

            def third(g, total, s=s, half=half):
                for k in range(16):
                    total = total + stored[s, g * 16 + k, half * 64 : half * 64 + 64] * band_b[s, pl.ds(g * 16 + k, 1), :]
                return total

            terms[s, half * 64 : half * 64 + 64, :] = lax.fori_loop(
                0, SIDE // 16, third, jnp.zeros((64, WIDTH), F32)
            )
        gather(2, half * 64, 64)
        send(
            C_SUMS, NX, peer_x, lambda d: rows_for(2, lax.rem(gx + d, NX), 16), lambda d: take_c.at[d - 1],
            when=lambda d, half=half: in_half(lax.rem(gx + d, NX), half),
        )

    received(GN_PART, parts_n)
    gram_n[piece, :] = gram_own[2, piece, :] + jnp.sum(parts_n[...], axis=0)
    send(GN_ALL, NG, peer_g, lambda d: gram_n.at[piece], lambda d: gram_n.at[piece])
    received(C_SUMS, take_c)
    here = pl.multiple_of(gx * 16, 16)
    last_c[NY - 1] = sums[2, pl.ds(here, 16), :] + jnp.sum(take_c[...], axis=0)
    send(C_LAST, NY, peer_y, lambda d: last_c.at[NY - 1], lambda d: last_c.at[d - 1])

    received(GN_ALL, gram_n.at[pl.ds(0, (NG - 1) * PIECE)])
    penalty, inverse = newton_inverse(gram_a[...], gram_n[...], p_ref, q_ref)
    received(C_LAST, last_c.at[pl.ds(0, NY - 1)])
    totals = jnp.sum(last_c[...], axis=0)
    start = slab_c[pl.ds(row_c, 16), :].astype(F32)
    updated = row_update(totals, start, penalty, inverse)
    chosen = [
        jnp.sum(jnp.where(lines == 2 * gy + k, updated, 0.0), axis=0, keepdims=True) for k in range(2)
    ]
    out_c[0] = jnp.concatenate(chosen, axis=0).astype(BF16)

    sent(B_ROWS, slab_b.at[pl.ds(0, NB - 1)])
    sent(C_NEAR, near_c.at[pl.ds(0, NY - 1)])
    sent(C_ROWS, slab_c.at[pl.ds(0, (NX - 1) * 16)])
    sent(C_OTHER, slab_c.at[half_c])
    sent(GB_PART, gram_part)
    sent(GB_ALL, gram_b.at[pl.ds(0, (NG - 1) * PIECE)])
    sent(A_SUMS, take_a)
    sent(A_ROWS, slab_a.at[pl.ds(0, (NA - 1) * 16)])
    sent(GA_PART, parts_a)
    sent(GA_ALL, halved.at[pl.ds(0, NA - 1)])
    sent(GA_DIAG, diagonals.at[pl.ds(0, NX - 1)])
    sent(B_SUMS, take_b)
    sent(B_NEW, new_b.at[pl.ds(0, NB - 1)])
    sent(GN_PART, parts_n)
    sent(GN_ALL, gram_n.at[pl.ds(0, (NG - 1) * PIECE)])
    sent(C_SUMS, take_c)
    sent(C_LAST, last_c.at[pl.ds(0, NY - 1)])


def hand_over(in_a, in_b, in_c, out_a, out_b, out_c):
    out_a[...] = in_a[...]
    out_b[...] = in_b[...]
    out_c[...] = in_c[...]


def on_device(tensor_blocks, block_coords, live_counts, factor_a, factor_b, factor_c):
    vmem = pl.BlockSpec(memory_space=pltpu.VMEM)
    smem = pl.BlockSpec(memory_space=pltpu.SMEM)
    square = pltpu.VMEM((WIDTH, WIDTH), F32)
    scratch = [
        pltpu.VMEM((2, SIDE, SIDE, SIDE), BF16),
        pltpu.VMEM((2, SIDE, SIDE, SIDE), BF16),
        pltpu.VMEM((2, SIDE, SIDE, WIDTH), F32),
        pltpu.VMEM((NB, 16, 128), BF16),
        square,
        pltpu.VMEM((NZ * SLAB, WIDTH), BF16),
        pltpu.VMEM((NY, 16, WIDTH), BF16),
        pltpu.VMEM((2, SIDE, WIDTH), F32),
        pltpu.VMEM((2, SIDE, WIDTH), BF16),
        pltpu.VMEM((2, SIDE, WIDTH), F32),
        pltpu.VMEM((3, SLAB, WIDTH), F32),
        pltpu.VMEM((2, SIDE, WIDTH), F32),
        pltpu.VMEM((3, WIDTH, WIDTH), F32),
        pltpu.VMEM((NY - 1, PIECE, WIDTH), F32),
        square,
        square,
        square,
        square,
        pltpu.VMEM((NX - 1, 16, 128), F32),
        pltpu.VMEM((NY - 1, PIECE, WIDTH), F32),
        pltpu.VMEM((NA, 16, 128), F32),
        pltpu.VMEM((NA, 16, 128), F32),
        pltpu.VMEM((NX, 8, 128), F32),
        pltpu.VMEM((NA - 1, 16, WIDTH), F32),
        pltpu.VMEM((SLAB, WIDTH), BF16),
        pltpu.VMEM((NB - 1, 8, WIDTH), F32),
        pltpu.VMEM((NB, 16, 128), BF16),
        pltpu.VMEM((NX - 1, 16, WIDTH), F32),
        pltpu.VMEM((NY, 16, WIDTH), F32),
        square,
        square,
        pltpu.SemaphoreType.DMA((2,)),
        pltpu.SemaphoreType.DMA((PHASES + 4,)),
        pltpu.SemaphoreType.DMA((PHASES + 4,)),
    ]
    shapes = tuple(jax.ShapeDtypeStruct(f.shape, BF16) for f in (factor_a, factor_b, factor_c))
    updated = pl.pallas_call(
        kernel,
        out_shape=shapes,
        in_specs=[smem, vmem, pl.BlockSpec(memory_space=pl.ANY), vmem, vmem, vmem],
        out_specs=(vmem, vmem, vmem),
        scratch_shapes=scratch,
        compiler_params=pltpu.CompilerParams(
            collective_id=0, has_side_effects=True, vmem_limit_bytes=60 * 1024 * 1024
        ),
        name="sweep",
    )(block_coords, live_counts, tensor_blocks, factor_a, factor_b, factor_c)
    return pl.pallas_call(
        hand_over, out_shape=shapes, in_specs=[vmem] * 3, out_specs=(vmem,) * 3, name="hand_over"
    )(*updated)


def solution(mesh):
    factors = (P("gx", ("gy", "gz"), None), P("gy", ("gx", "gz"), None), P("gz", ("gx", "gy"), None))
    return jax.shard_map(
        on_device,
        mesh=mesh,
        in_specs=(P("gx", "gy", "gz"), P("gx", "gy", "gz"), P("gx", "gy", "gz"), *factors),
        out_specs=factors,
        check_vma=False,
    )
```

```python
import functools

import jax
import jax.numpy as jnp
from jax import lax
from jax.experimental import pallas as pl
from jax.experimental.pallas import tpu as pltpu
from jax.sharding import PartitionSpec as P

NS_STEPS = 8
ADMM_ITERS = 4
SIDE = 128
WIDTH = 256
SLAB = 256
NX, NY, NZ = 16, 8, 2
NA = NY * NZ
NB = NX * NZ
LINE = 4
NG = LINE * NZ
PIECE = WIDTH // NG
F32 = jnp.float32
BF16 = jnp.bfloat16
MESH = pl.DeviceIdType.MESH
PHASES = 13
(B_ROWS, C_NEAR, C_ROWS, GB_PART, GB_ALL, A_SUMS, A_ROWS, GA_PART, GA_ALL, B_SUMS, B_NEW, GN_PART, GN_ALL) = range(PHASES)
C_SUMS, C_LAST, C_OTHER, GA_DIAG = PHASES, PHASES + 1, PHASES + 2, PHASES + 3


def split(x):
    high = x.astype(BF16)
    return high, (x - high.astype(F32)).astype(BF16)


def dot(a, b):
    return jnp.dot(a, b, preferred_element_type=F32)


def dot_first(a, b):
    return lax.dot_general(a, b, (((0,), (0,)), ((), ())), preferred_element_type=F32)


def dot_split(a, b):
    return dot(a[0], b[0]) + (dot(a[0], b[1]) + dot(a[1], b[0]))


def newton_inverse(gram_left, gram_right, p_ref, q_ref):
    rows = lax.broadcasted_iota(jnp.int32, (WIDTH, WIDTH), 0)
    columns = lax.broadcasted_iota(jnp.int32, (WIDTH, WIDTH), 1)
    eye = rows == columns
    weighted = gram_left * gram_right
    diagonal = jnp.sum(jnp.where(eye, weighted, 0.0), axis=0, keepdims=True)
    penalty = jnp.sum(diagonal, axis=1, keepdims=True) / WIDTH
    system = weighted + jnp.where(eye, penalty, 0.0)
    bound = jnp.max(jnp.sum(jnp.abs(system), axis=0, keepdims=True), axis=1, keepdims=True)
    q = system / bound
    p_ref[...] = jnp.where(eye, 2.0, 0.0) - q
    halves = split(q)
    q_ref[...] = 2.0 * q - dot_split(halves, halves)

    def step(t, carry):
        q = q_ref[...]
        p = p_ref[...]
        right = split(q)
        p_ref[...] = 2.0 * p - dot_split(split(p), right)
        q_ref[...] = 2.0 * q - dot_split(right, right)
        return carry

    lax.fori_loop(0, NS_STEPS - 2, step, 0)
    p = p_ref[...]
    inverse = (2.0 * p - dot_split(split(p), split(q_ref[...]))) / bound
    return penalty, split(inverse)


def row_update(totals, start, penalty, inverse):
    count = start.shape[0]
    primal = start
    dual = jnp.zeros_like(primal)
    for step in range(ADMM_ITERS):
        value = totals + penalty * (primal + dual)
        high = value.astype(BF16).astype(F32)
        both = dot(jnp.concatenate([high, value - high], axis=0).astype(BF16), inverse[0])
        target = both[:count] + (both[count:] + dot(high.astype(BF16), inverse[1]))
        primal = jnp.maximum(target - dual, 0.0)
        dual = dual + primal - target
    return primal


def packed(x):
    count = x.shape[0] // 8
    left = x[:, :128].reshape(count, 8, 128)
    right = x[:, 128:].reshape(count, 8, 128)
    return jnp.concatenate([left, right], axis=1)


def unpacked(x):
    count = x.shape[0]
    left = x[:, :8, :].reshape(count * 8, 128)
    right = x[:, 8:, :].reshape(count * 8, 128)
    return jnp.concatenate([left, right], axis=1)


def kernel(
    coords, live, x_hbm, own_a, own_b, own_c, out_a, out_b, out_c,
    x, turned, stored, slab_b, slab_b32, slab_c, near_c, band_b, band_c, band_a, sums, terms,
    gram_own, gram_part, gram_b, gram_c, gram_a, gram_n, parts_a, parts_n,
    halved_own, halved, diagonals,
    take_a, slab_a, take_b, new_b, take_c, last_c, p_ref, q_ref,
    x_sem, send_sem, recv_sem,
):
    gx, gy, gz = lax.axis_index("gx"), lax.axis_index("gy"), lax.axis_index("gz")
    at_a = gy * NZ + gz
    at_b = gx * NZ + gz

    def peer_a(d):
        other = lax.rem(at_a + d, NA)
        return (gx, lax.div(other, NZ), lax.rem(other, NZ))

    def peer_b(d):
        other = lax.rem(at_b + d, NB)
        return (lax.div(other, NZ), gy, lax.rem(other, NZ))

    at_g = lax.rem(gx, LINE) * NZ + gz

    def peer_g(d):
        other = lax.rem(at_g + d, NG)
        return (lax.div(gx, LINE) * LINE + lax.div(other, NZ), gy, lax.rem(other, NZ))

    def peer_x(d):
        return (lax.rem(gx + d, NX), gy, gz)

    def peer_z(d):
        return (gx, gy, lax.rem(gz + d, NZ))

    def peer_y(d):
        return (gx, lax.rem(gy + d, NY), gz)

    def send(phase, count, peer, source, target, when=None):
        def start(d):
            pltpu.make_async_remote_copy(
                src_ref=source(d), dst_ref=target(d), send_sem=send_sem.at[phase],
                recv_sem=recv_sem.at[phase], device_id=peer(d), device_id_type=MESH,
            ).start()

        def one(d, carry):
            if when is None:
                start(d)
            else:
                pl.when(when(d))(lambda: start(d))
            return carry

        lax.fori_loop(1, count, one, 0)

    def received(phase, ref):
        pltpu.make_async_copy(ref, ref, recv_sem.at[phase]).wait()

    def sent(phase, ref):
        pltpu.make_async_copy(ref, ref, send_sem.at[phase]).wait()

    loads = [pltpu.make_async_copy(x_hbm.at[0, 0, 0, s], x.at[s], x_sem.at[s]) for s in range(2)]
    for load in loads:
        load.start()

    barrier = pltpu.get_barrier_semaphore()

    def greet(peer):
        def one(d, carry):
            pl.semaphore_signal(barrier, inc=1, device_id=peer(d), device_id_type=MESH)
            return carry

        return one

    lax.fori_loop(1, NB, greet(peer_b), 0)
    lax.fori_loop(1, NA, greet(peer_a), 0)

    slab_b[at_b] = packed(own_b[0].astype(F32))[0].astype(BF16)
    rows_c = own_c[0].astype(F32)
    lines = lax.broadcasted_iota(jnp.int32, (16, WIDTH), 0)
    mine_c = lax.div(lines, 2) == gy
    placed = jnp.where(mine_c, jnp.where(lax.rem(lines, 2) == 0, rows_c[0:1], rows_c[1:2]), 0.0)
    near_c[NY - 1] = placed.astype(BF16)
    flags = [[coords[0, 0, 0, s, m].astype(F32) for m in range(3)] for s in range(2)]
    alive = [(live[0] > s).astype(jnp.int32).astype(F32) for s in range(2)]

    def turn(s):
        loads[s].wait()

        def one(g, carry):
            at = pl.multiple_of(g * 16, 16)
            turned[s, :, pl.ds(at, 16), :] = jnp.swapaxes(x[s, pl.ds(at, 16)], 0, 1)
            return carry

        lax.fori_loop(0, SIDE // 16, one, 0)

    pl.semaphore_wait(barrier, NA + NB - 2)

    def banded(slot, mode, ref, offset):
        flag = flags[slot][mode]
        low = ref[offset : offset + SIDE, :].astype(F32)
        high = ref[offset + SIDE : offset + 2 * SIDE, :].astype(F32)
        return low * (1.0 - flag) + high * flag

    send(C_NEAR, NY, peer_y, lambda d: near_c.at[NY - 1], lambda d: near_c.at[d - 1])
    send(B_ROWS, NB, peer_b, lambda d: slab_b.at[at_b], lambda d: slab_b.at[at_b])
    turn(0)
    received(C_NEAR, near_c.at[pl.ds(0, NY - 1)])
    sixteen_c = jnp.sum(near_c[...].astype(F32), axis=0)
    row_c = pl.multiple_of(gz * SLAB + gx * 16, 16)
    slab_c[pl.ds(row_c, 16), :] = sixteen_c.astype(BF16)
    send(C_ROWS, NX, peer_x, lambda d: slab_c.at[pl.ds(row_c, 16)], lambda d: slab_c.at[pl.ds(row_c, 16)])

    turn(1)

    received(B_ROWS, slab_b.at[pl.ds(0, NB - 1)])
    wide_b = unpacked(slab_b[...].astype(F32))
    slab_b32[...] = wide_b
    narrow_b = wide_b.astype(BF16)
    gram_own[0] = dot_first(narrow_b, narrow_b)
    row_b = pl.multiple_of(at_b * 8, 8)
    piece = pl.ds(pl.multiple_of(at_g * PIECE, PIECE), PIECE)
    send(GB_PART, NY, peer_y, lambda d: gram_own.at[0, piece], lambda d: gram_part.at[d - 1])
    for s in range(2):
        band_b[s] = banded(s, 1, slab_b32, 0)

    received(C_ROWS, slab_c.at[pl.ds(0, (NX - 1) * 16)])
    half_c = pl.ds(pl.multiple_of(gz * SLAB, SLAB), SLAB)
    send(C_OTHER, NZ, peer_z, lambda d: slab_c.at[half_c], lambda d: slab_c.at[half_c])
    slab_of_c = slab_c[half_c, :].astype(F32)
    for s in range(2):
        flag = flags[s][2]
        band_c[s] = (slab_of_c[:SIDE] * (1.0 - flag) + slab_of_c[SIDE:] * flag).astype(BF16)

    def gather(mode, start, count):
        for h in range(2):
            total = jnp.zeros((count, WIDTH), F32)
            for s in range(2):
                flag = flags[s][mode]
                weight = alive[s] * (flag if h else 1.0 - flag)
                total = total + terms[s, start : start + count, :] * weight
            sums[mode, h * SIDE + start : h * SIDE + start + count, :] = total

    def rows_for(mode, owner, count):
        return sums.at[mode, pl.ds(pl.multiple_of(owner * count, count), count)]

    def in_half(owner, half):
        return lax.div(lax.rem(owner, 8), 4) == half

    for half in range(2):
        for s in range(2):
            right = band_c[s]

            for at in range(half * 64, half * 64 + 64, 8):
                left = x[s, at : at + 8].reshape(8 * SIDE, SIDE)
                product = dot(left, right).reshape(8, SIDE, WIDTH)
                stored[s, at : at + 8] = product
                terms[s, at : at + 8, :] = jnp.sum(product * band_b[s][None], axis=1)
            if half == 0 and s == 0:
                received(GB_PART, gram_part)
                gram_b[piece, :] = gram_own[0, piece, :] + jnp.sum(gram_part[...], axis=0)
                send(GB_ALL, NG, peer_g, lambda d: gram_b.at[piece], lambda d: gram_b.at[piece])
        gather(0, half * 64, 64)
        send(
            A_SUMS, NA, peer_a, lambda d: rows_for(0, lax.rem(at_a + d, NA), 16), lambda d: take_a.at[d - 1],
            when=lambda d, half=half: in_half(lax.rem(at_a + d, NA), half),
        )

    received(C_OTHER, slab_c.at[half_c])
    whole_c = slab_c[...]
    gram_c[...] = dot_first(whole_c, whole_c)
    received(GB_ALL, gram_b.at[pl.ds(0, (NG - 1) * PIECE)])
    penalty, inverse = newton_inverse(gram_b[...], gram_c[...], p_ref, q_ref)
    received(A_SUMS, take_a)
    row_a = pl.multiple_of(at_a * 16, 16)
    totals = sums[0, pl.ds(row_a, 16), :] + jnp.sum(take_a[...], axis=0)
    updated = row_update(totals, own_a[0].astype(F32), penalty, inverse).astype(BF16)
    out_a[0] = updated
    slab_a[pl.ds(row_a, 16), :] = updated
    send(A_ROWS, NA, peer_a, lambda d: slab_a.at[pl.ds(row_a, 16)], lambda d: slab_a.at[pl.ds(row_a, 16)])

    received(A_ROWS, slab_a.at[pl.ds(0, (NA - 1) * 16)])
    narrow_a = slab_a[...]
    whole = dot_first(narrow_a, narrow_a)
    across = lax.broadcasted_iota(jnp.int32, (128, 128), 1)
    down = lax.broadcasted_iota(jnp.int32, (128, 128), 0)
    last = whole[128:, 128:]
    mixed = jnp.where(across >= down, whole[:128, :128], last)
    halved_own[:, :8, :] = whole[:128, 128:].reshape(NA, 8, 128)
    halved_own[:, 8:, :] = mixed.reshape(NA, 8, 128)
    diagonal = jnp.sum(jnp.where(across == down, last, 0.0), axis=0, keepdims=True)
    diagonals[NX - 1] = diagonal
    send(GA_PART, NX, peer_x, lambda d: halved_own.at[at_a], lambda d: parts_a.at[d - 1])
    send(GA_DIAG, NX, peer_x, lambda d: diagonals.at[NX - 1], lambda d: diagonals.at[d - 1])

    for s in range(2):
        band_a[s] = banded(s, 0, slab_a, 0)
    for half in range(2):
        rows = slice(half * 64, half * 64 + 64)
        for s in range(2):

            def second(g, total, s=s, rows=rows):
                for k in range(16):
                    total = total + stored[s, g * 16 + k, rows] * band_a[s, pl.ds(g * 16 + k, 1), :]
                return total

            terms[s, rows, :] = lax.fori_loop(0, SIDE // 16, second, jnp.zeros((64, WIDTH), F32))
    gather(1, 0, SIDE)
    send(B_SUMS, NB, peer_b, lambda d: rows_for(1, lax.rem(at_b + d, NB), 8), lambda d: take_b.at[d - 1])

    def product_a(s, start, steps):
        right = band_a[s].astype(BF16)

        def one(g, carry):
            for k in range(32):
                at = start + g * 32 + k
                stored[s, at] = dot_first(turned[s, at], right)
            return carry

        lax.fori_loop(0, steps, one, 0)

    product_a(0, 0, 1)

    received(GA_PART, parts_a)
    halved[at_a] = halved_own[at_a] + jnp.sum(parts_a[...], axis=0)
    send(GA_ALL, NA, peer_a, lambda d: halved.at[at_a], lambda d: halved.at[at_a])
    received(GA_DIAG, diagonals.at[pl.ds(0, NX - 1)])
    diagonal = jnp.sum(diagonals[...], axis=0)
    product_a(0, 32, 3)
    received(GA_ALL, halved.at[pl.ds(0, NA - 1)])
    corner = halved[:, :8, :].reshape(128, 128)
    mixed = halved[:, 8:, :].reshape(128, 128)
    flipped = mixed.T
    gram_a[:128, :128] = jnp.where(across >= down, mixed, flipped)
    gram_a[:128, 128:] = corner
    gram_a[128:, :128] = corner.T
    gram_a[128:, 128:] = jnp.where(across < down, mixed, jnp.where(across > down, flipped, diagonal))

    penalty, inverse = newton_inverse(gram_a[...], gram_c[...], p_ref, q_ref)
    received(B_SUMS, take_b)
    totals = sums[1, pl.ds(row_b, 8), :] + jnp.sum(take_b[...], axis=0)
    updated = row_update(totals, own_b[0].astype(F32), penalty, inverse)
    out_b[0] = updated.astype(BF16)
    new_b[at_b] = packed(updated)[0].astype(BF16)
    send(B_NEW, NB, peer_b, lambda d: new_b.at[at_b], lambda d: new_b.at[at_b])
    product_a(1, 0, 4)

    received(B_NEW, new_b.at[pl.ds(0, NB - 1)])
    wide_b = unpacked(new_b[...].astype(F32))
    slab_b32[...] = wide_b
    narrow_b = wide_b.astype(BF16)
    gram_own[2] = dot_first(narrow_b, narrow_b)
    send(GN_PART, NY, peer_y, lambda d: gram_own.at[2, piece], lambda d: parts_n.at[d - 1])

    for s in range(2):
        band_b[s] = banded(s, 1, slab_b32, 0)
    for half in range(2):
        for s in range(2):

            def third(g, total, s=s, half=half):
                for k in range(16):
                    total = total + stored[s, g * 16 + k, half * 64 : half * 64 + 64] * band_b[s, pl.ds(g * 16 + k, 1), :]
                return total

            terms[s, half * 64 : half * 64 + 64, :] = lax.fori_loop(
                0, SIDE // 16, third, jnp.zeros((64, WIDTH), F32)
            )
        gather(2, half * 64, 64)
        send(
            C_SUMS, NX, peer_x, lambda d: rows_for(2, lax.rem(gx + d, NX), 16), lambda d: take_c.at[d - 1],
            when=lambda d, half=half: in_half(lax.rem(gx + d, NX), half),
        )

    received(GN_PART, parts_n)
    gram_n[piece, :] = gram_own[2, piece, :] + jnp.sum(parts_n[...], axis=0)
    send(GN_ALL, NG, peer_g, lambda d: gram_n.at[piece], lambda d: gram_n.at[piece])
    received(C_SUMS, take_c)
    here = pl.multiple_of(gx * 16, 16)
    last_c[NY - 1] = sums[2, pl.ds(here, 16), :] + jnp.sum(take_c[...], axis=0)
    send(C_LAST, NY, peer_y, lambda d: last_c.at[NY - 1], lambda d: last_c.at[d - 1])

    received(GN_ALL, gram_n.at[pl.ds(0, (NG - 1) * PIECE)])
    penalty, inverse = newton_inverse(gram_a[...], gram_n[...], p_ref, q_ref)
    received(C_LAST, last_c.at[pl.ds(0, NY - 1)])
    totals = jnp.sum(last_c[...], axis=0)
    start = slab_c[pl.ds(row_c, 16), :].astype(F32)
    updated = row_update(totals, start, penalty, inverse)
    chosen = [
        jnp.sum(jnp.where(lines == 2 * gy + k, updated, 0.0), axis=0, keepdims=True) for k in range(2)
    ]
    out_c[0] = jnp.concatenate(chosen, axis=0).astype(BF16)

    sent(B_ROWS, slab_b.at[pl.ds(0, NB - 1)])
    sent(C_NEAR, near_c.at[pl.ds(0, NY - 1)])
    sent(C_ROWS, slab_c.at[pl.ds(0, (NX - 1) * 16)])
    sent(C_OTHER, slab_c.at[half_c])
    sent(GB_PART, gram_part)
    sent(GB_ALL, gram_b.at[pl.ds(0, (NG - 1) * PIECE)])
    sent(A_SUMS, take_a)
    sent(A_ROWS, slab_a.at[pl.ds(0, (NA - 1) * 16)])
    sent(GA_PART, parts_a)
    sent(GA_ALL, halved.at[pl.ds(0, NA - 1)])
    sent(GA_DIAG, diagonals.at[pl.ds(0, NX - 1)])
    sent(B_SUMS, take_b)
    sent(B_NEW, new_b.at[pl.ds(0, NB - 1)])
    sent(GN_PART, parts_n)
    sent(GN_ALL, gram_n.at[pl.ds(0, (NG - 1) * PIECE)])
    sent(C_SUMS, take_c)
    sent(C_LAST, last_c.at[pl.ds(0, NY - 1)])


def hand_over(in_a, in_b, in_c, out_a, out_b, out_c):
    out_a[...] = in_a[...]
    out_b[...] = in_b[...]
    out_c[...] = in_c[...]


def on_device(tensor_blocks, block_coords, live_counts, factor_a, factor_b, factor_c):
    vmem = pl.BlockSpec(memory_space=pltpu.VMEM)
    smem = pl.BlockSpec(memory_space=pltpu.SMEM)
    square = pltpu.VMEM((WIDTH, WIDTH), F32)
    scratch = [
        pltpu.VMEM((2, SIDE, SIDE, SIDE), BF16),
        pltpu.VMEM((2, SIDE, SIDE, SIDE), BF16),
        pltpu.VMEM((2, SIDE, SIDE, WIDTH), F32),
        pltpu.VMEM((NB, 16, 128), BF16),
        square,
        pltpu.VMEM((NZ * SLAB, WIDTH), BF16),
        pltpu.VMEM((NY, 16, WIDTH), BF16),
        pltpu.VMEM((2, SIDE, WIDTH), F32),
        pltpu.VMEM((2, SIDE, WIDTH), BF16),
        pltpu.VMEM((2, SIDE, WIDTH), F32),
        pltpu.VMEM((3, SLAB, WIDTH), F32),
        pltpu.VMEM((2, SIDE, WIDTH), F32),
        pltpu.VMEM((3, WIDTH, WIDTH), F32),
        pltpu.VMEM((NY - 1, PIECE, WIDTH), F32),
        square,
        square,
        square,
        square,
        pltpu.VMEM((NX - 1, 16, 128), F32),
        pltpu.VMEM((NY - 1, PIECE, WIDTH), F32),
        pltpu.VMEM((NA, 16, 128), F32),
        pltpu.VMEM((NA, 16, 128), F32),
        pltpu.VMEM((NX, 1, 128), F32),
        pltpu.VMEM((NA - 1, 16, WIDTH), F32),
        pltpu.VMEM((SLAB, WIDTH), BF16),
        pltpu.VMEM((NB - 1, 8, WIDTH), F32),
        pltpu.VMEM((NB, 16, 128), BF16),
        pltpu.VMEM((NX - 1, 16, WIDTH), F32),
        pltpu.VMEM((NY, 16, WIDTH), F32),
        square,
        square,
        pltpu.SemaphoreType.DMA((2,)),
        pltpu.SemaphoreType.DMA((PHASES + 4,)),
        pltpu.SemaphoreType.DMA((PHASES + 4,)),
    ]
    shapes = tuple(jax.ShapeDtypeStruct(f.shape, BF16) for f in (factor_a, factor_b, factor_c))
    updated = pl.pallas_call(
        kernel,
        out_shape=shapes,
        in_specs=[smem, vmem, pl.BlockSpec(memory_space=pl.ANY), vmem, vmem, vmem],
        out_specs=(vmem, vmem, vmem),
        scratch_shapes=scratch,
        compiler_params=pltpu.CompilerParams(
            collective_id=0, has_side_effects=True, vmem_limit_bytes=60 * 1024 * 1024
        ),
        name="sweep",
    )(block_coords, live_counts, tensor_blocks, factor_a, factor_b, factor_c)
    return pl.pallas_call(
        hand_over, out_shape=shapes, in_specs=[vmem] * 3, out_specs=(vmem,) * 3, name="hand_over"
    )(*updated)


def solution(mesh):
    factors = (P("gx", ("gy", "gz"), None), P("gy", ("gx", "gz"), None), P("gz", ("gx", "gy"), None))
    return jax.shard_map(
        on_device,
        mesh=mesh,
        in_specs=(P("gx", "gy", "gz"), P("gx", "gy", "gz"), P("gx", "gy", "gz"), *factors),
        out_specs=factors,
        check_vma=False,
    )
```
